256 devices in a mesh: dp: 256 (over y, z, x, core).
Axes of the slice: x: 4, y: 4, z: 8, core: 2. Of those that a mesh axis runs over, the one named last changes fastest.
Arguments:
- queries: bfloat16 [2048, 32, 128], P('dp')
- pages: bfloat16 [512, 1030, 128], P('dp')
- counts: int32 [512], P('dp'), may hold values from 700 to 1030
- labels: int32 [2048], P('dp'), may hold values from 0 to 511, as said below
- logit_scale: float32 [], replicated, may hold values from 0.02 to 0.1
- logit_bias: float32 [], replicated, may hold values from -6 to -1
Outputs:
- loss_total: float32 [], replicated
- grad_queries: float32 [2048, 32, 128], P('dp')
- grad_pages: float32 [512, 1030, 128], P('dp')
The draws below stay inside these ranges and needn't reach their ends.
Inputs may be any that keep to these rules, and one draw needn't show every extreme that they name: `labels`: each query's positive page is one of the pages it is scored with.
All inputs are finite; a program needn't handle non-finite values.
Results may differ from the reference program's by a relative error of at most 0.0028.
Values may be sent and summed in bfloat16 or wider, within the bound.
A program may use at most 64 MiB of HBM per device.

```python
import math
import jax
import jax.numpy as jnp
from jax import lax

EMB = 128
PT = 1030
QT = 32
ROUNDS = 4
P_DEV = 2
Q_DEV = 8
PAGES = 512
QUERIES = 2048
N_DP = 256


def anchor_rows(key):
    return 0.25 * jax.random.normal(jax.random.fold_in(key, 101), (PAGES, EMB), jnp.float32)


def label_pages(key):
    label_key = jax.random.fold_in(key, 202)
    devices = PAGES // P_DEV
    log_count = devices.bit_length() - 1
    query_ids = jnp.arange(QUERIES, dtype=jnp.int32)
    home = query_ids // Q_DEV
    picked = jax.random.randint(jax.random.fold_in(label_key, 1), (QUERIES,), 0, ROUNDS + 1, dtype=jnp.int32)
    shifted = jnp.where(picked > 0, jnp.left_shift(jnp.int32(1), jnp.maximum(log_count - picked, 0)), 0)
    partner = jnp.bitwise_xor(home, shifted.astype(jnp.int32))
    slot_ids = jax.random.randint(jax.random.fold_in(label_key, 2), (QUERIES,), 0, P_DEV, dtype=jnp.int32)
    chosen = (partner * P_DEV + slot_ids).astype(jnp.int32)
    chosen = jnp.where(query_ids == 0, jnp.int32(0), chosen)
    chosen = jnp.where(query_ids == QUERIES - 1, jnp.int32(PAGES - 1), chosen)
    return chosen.astype(jnp.int32)


def rising_scale(low, high):
    query_ids = jnp.arange(QUERIES, dtype=jnp.float32)
    return low + (high - low) * query_ids / max(QUERIES - 1, 1)


def draw_labels(key, part):
    return label_pages(key)


def draw_pages(key, part):
    anchors = anchor_rows(key)
    key = jax.random.fold_in(key, 1)
    base = 0.25 * jax.random.normal(key, (PAGES, PT, EMB), jnp.float32)
    base = base.at[:, 0, :].set(anchors)
    return base.astype(jnp.bfloat16)


def draw_queries(key, part):
    key = jax.random.fold_in(key, 2)
    base = 0.25 * jax.random.normal(key, (QUERIES, QT, EMB), jnp.float32)
    base = base * rising_scale(0.5, 2.0)[:, None, None]
    return base.astype(jnp.bfloat16)


def plant(result, own_key, smallest, largest):
    longest = result.shape.index(max(result.shape))
    spots = []
    for shift in (0, 1):
        where = [jax.random.randint(jax.random.fold_in(own_key, axis), (), 0, length) for axis, length in enumerate(result.shape)]
        where[longest] = (where[longest] + shift) % result.shape[longest]
        spots.append(tuple(where))
    return result.at[spots[0]].set(smallest).at[spots[1]].set(largest)


def setup_inputs(seed: int = 0) -> dict:
    keys = jax.random.split(jax.random.key(seed), 7)
    queries = draw_queries(jax.random.fold_in(keys[6], 71), 0)
    pages = draw_pages(jax.random.fold_in(keys[6], 71), 0)
    counts = plant(jax.random.randint(keys[2], (PAGES,), (PT * 17) // 25, PT + 1), jax.random.fold_in(keys[2], 1), (PT * 17) // 25, PT).astype(jnp.int32)
    labels = draw_labels(jax.random.fold_in(keys[6], 71), 0)
    logit_scale = jnp.clip(jnp.exp(jax.random.uniform(keys[4], (), jnp.float32, math.log(0.02), math.log(0.1))), 0.02, 0.1)
    logit_bias = jnp.clip(jax.random.uniform(keys[5], (), jnp.float32, -6.0, -1.0), -6.0, -1.0)
    return {"queries": queries, "pages": pages, "counts": counts, "labels": labels, "logit_scale": logit_scale, "logit_bias": logit_bias}


SOFTMAX_WARMTH = 0.1


def block_terms(query_block, page_block, page_mask, targets, logit_scale, logit_bias):
    n_query, q_tok, emb_width = query_block.shape
    flat_query = query_block.reshape(n_query * q_tok, emb_width)

    def one_page(page_items):
        page_rows, valid_row, target_col = page_items
        match_scores = lax.dot_general(flat_query, page_rows, (((1,), (1,)), ((), ())), preferred_element_type=jnp.float32)
        retained_mask = valid_row[None, :] > 0
        row_maximum = jnp.max(jnp.where(retained_mask, match_scores, -jnp.inf), axis=1, keepdims=True)
        power_term = jnp.where(retained_mask, jnp.exp((match_scores - row_maximum) / SOFTMAX_WARMTH), 0.0)
        row_summation = jnp.sum(power_term, axis=1, keepdims=True)
        weights = power_term / row_summation
        smoothed_maximum = row_maximum[:, 0] + SOFTMAX_WARMTH * jnp.log(row_summation[:, 0])
        page_score = jnp.sum(smoothed_maximum.reshape(n_query, q_tok), axis=1)
        logits_now = logit_scale * page_score + logit_bias
        sign_vals = 2.0 * target_col.astype(jnp.float32) - 1.0
        pair_loss = jnp.sum(jax.nn.softplus(-sign_vals * logits_now))
        slopes = -sign_vals * logit_scale * jax.nn.sigmoid(-sign_vals * logits_now)
        coefficient = (weights * jnp.repeat(slopes, q_tok)[:, None]).astype(jnp.bfloat16)
        grad_rows = jnp.dot(coefficient, page_rows, preferred_element_type=jnp.float32)
        grad_page = lax.dot_general(coefficient, flat_query, (((0,), (0,)), ((), ())), preferred_element_type=jnp.float32)
        return pair_loss, grad_rows, grad_page

    losses, grad_rows, grad_pages = lax.map(one_page, (page_block, page_mask, targets.T))
    return jnp.sum(losses), jnp.sum(grad_rows, axis=0).reshape(n_query, q_tok, emb_width), grad_pages


def reference(queries, pages, counts, labels, logit_scale, logit_bias):
    log_count = N_DP.bit_length() - 1
    positions = jnp.arange(PT, dtype=jnp.int32)
    page_mask = (positions[None, :] < counts[:, None]).astype(jnp.bfloat16)
    offsets = jnp.arange(P_DEV, dtype=jnp.int32)

    def per_device(carry, device):
        grad_pages, loss_sum = carry
        query_block = lax.dynamic_slice_in_dim(queries, (device * Q_DEV).astype(jnp.int32), Q_DEV, 0)
        label_block = lax.dynamic_slice_in_dim(labels, (device * Q_DEV).astype(jnp.int32), Q_DEV, 0)
        grad_query = jnp.zeros((Q_DEV, QT, EMB), jnp.float32)
        for round_number in range(ROUNDS + 1):
            if round_number == 0:
                partner = device
            else:
                partner = jnp.bitwise_xor(device, jnp.int32(1 << (log_count - round_number)))
            start = (partner * P_DEV).astype(jnp.int32)
            page_block = lax.dynamic_slice_in_dim(pages, start, P_DEV, 0)
            mask_block = lax.dynamic_slice_in_dim(page_mask, start, P_DEV, 0)
            targets = (label_block[:, None] == start + offsets[None, :]).astype(jnp.float32)
            block_loss, block_rows, block_pages = block_terms(query_block, page_block, mask_block, targets, logit_scale, logit_bias)
            loss_sum = loss_sum + block_loss
            grad_query = grad_query + block_rows
            current = lax.dynamic_slice_in_dim(grad_pages, start, P_DEV, 0)
            grad_pages = lax.dynamic_update_slice_in_dim(grad_pages, current + block_pages, start, 0)
        return (grad_pages, loss_sum), grad_query

    init = (jnp.zeros((PAGES, PT, EMB), jnp.float32), jnp.zeros((), jnp.float32))
    (grad_pages, loss_sum), grad_queries = lax.scan(per_device, init, jnp.arange(N_DP, dtype=jnp.int32))
    return loss_sum, grad_queries.reshape(QUERIES, QT, EMB), grad_pages
```

```python
import jax
import jax.numpy as jnp
from jax import lax
from jax.experimental import pallas as pl
from jax.experimental.pallas import tpu as pltpu
from jax.sharding import PartitionSpec as P

EMB = 128
QT = 32
TAU = 0.1
EXP2_SCALE = 1.4426950408889634 / TAU
MIN_COUNT = 700
MESH = pl.DeviceIdType.MESH


def kernel(
    n_dev, q_rows, p_rows,
    q_hbm, p_hbm, counts, labels, scale, bias,
    loss_out, gq_out, gp_out,
    qbuf, pg, pgt, xs, gown, gsend, grecv, ones, lvec, lsend, l1, l2,
    local_sem, q_send, q_recv, g_send, g_recv, l_send, l_recv,
):
    me = lax.axis_index("dp")
    n_bits = n_dev.bit_length() - 1
    flip = [(1 << b) - 2 * (1 << b) * ((me // (1 << b)) % 2) for b in range(n_bits)]
    low_bits = n_bits - 4

    def peer(offset):
        out = me
        for b in range(n_bits):
            if offset >> b & 1:
                out = out + flip[b]
        return out

    group_a = [d << low_bits for d in range(1, 16)]
    group_b = list(range(1, 1 << low_bits))
    bits = [n_bits - 2, n_bits - 4, n_bits - 1, n_bits - 3]
    p_pad = pg.shape[0]

    barrier = pltpu.get_barrier_semaphore()
    for d in group_a + group_b:
        pl.semaphore_signal(barrier, inc=1, device_id=(peer(d),), device_id_type=MESH)

    get_q = pltpu.make_async_copy(q_hbm, qbuf.at[0, pl.ds(0, q_rows)], local_sem.at[0])
    get_q.start()
    pg[pl.ds(p_pad - 16, 16), :] = jnp.zeros((16, EMB), jnp.bfloat16)
    get_p = pltpu.make_async_copy(p_hbm.reshape(p_rows, EMB), pg.at[pl.ds(0, p_rows)], local_sem.at[1])
    get_p.start()

    row = lax.broadcasted_iota(jnp.int32, (16, EMB), 0)
    lane = lax.broadcasted_iota(jnp.int32, (16, EMB), 1)
    which = (row & 1) * (EMB // QT) + lane // QT
    label = jnp.zeros((16, EMB), jnp.int32)
    for q in range(q_rows // QT):
        label = jnp.where(which == q, labels[q], label)
    tail = jnp.where(row < 2, label >> 1, label & 1)
    qbuf[0, pl.ds(q_rows, 16), :] = tail.astype(jnp.float32).astype(jnp.bfloat16)

    get_q.wait()
    pl.semaphore_wait(barrier, len(group_a) + len(group_b))

    def q_copy(slot):
        return pltpu.make_async_remote_copy(
            qbuf.at[0], qbuf.at[slot], q_send.at[slot], q_recv.at[slot],
            device_id=(peer(1 << bits[slot - 1]),), device_id_type=MESH,
        )

    q_copies = {slot: q_copy(slot) for slot in (4, 2, 3, 1)}
    for copy in q_copies.values():
        copy.start()

    group_row = lax.broadcasted_iota(jnp.int32, (q_rows, q_rows), 0) // QT
    group_col = lax.broadcasted_iota(jnp.int32, (q_rows, q_rows), 1) // QT
    ones[...] = jnp.where(group_row == group_col, 1.0, 0.0).astype(jnp.bfloat16)
    gp2 = gp_out.reshape(p_rows, EMB)
    main_rows = p_rows // 16 * 16
    sub = lax.broadcasted_iota(jnp.int32, (8, q_rows), 0)
    parity = sub & 1
    limit = 2 * jnp.where(parity == 0, counts[0], counts[1]) - sub
    scale_v = scale[0]
    bias_v = bias[0]
    lvec[...] = jnp.zeros_like(lvec)

    chunk = p_pad // 3
    get_p.wait()
    for c in range(3):
        pgt[c] = pg[pl.ds(c * chunk, chunk), :].astype(jnp.float32).T.astype(jnp.bfloat16)

    def all_rows(vec, op):
        vec = op(vec, pltpu.roll(vec, 2, 0))
        return op(vec, pltpu.roll(vec, 4, 0))

    def forward(k):
        q = qbuf[k, pl.ds(0, q_rows), :]
        top = jnp.full((8, q_rows), -jnp.inf, jnp.float32)
        for c in range(3):
            x = lax.dot_general(
                pg[pl.ds(c * chunk, chunk), :], q, (((1,), (1,)), ((), ())), preferred_element_type=jnp.float32
            ).reshape(chunk // 8, 8, q_rows)
            if (c + 1) * chunk > 2 * MIN_COUNT:
                start = c * chunk + 8 * lax.broadcasted_iota(jnp.int32, x.shape, 0)
                x = jnp.where(limit[None] > start, x, -jnp.inf)
            xs[c] = x
            top = jnp.maximum(top, jnp.max(x, axis=0))
        top = all_rows(top, jnp.maximum)
        total = jnp.zeros((8, q_rows), jnp.float32)
        for c in range(3):
            e = jnp.exp2((xs[c] - top[None]) * EXP2_SCALE)
            xs[c] = e
            total = total + jnp.sum(e, axis=0)
        total = all_rows(total, jnp.add)
        soft = top + TAU * jnp.log(total)
        hi = soft.astype(jnp.bfloat16).astype(jnp.float32)
        rest = soft - hi
        mid = rest.astype(jnp.bfloat16).astype(jnp.float32)
        parts = jnp.concatenate([hi, mid, rest - mid, jnp.zeros_like(hi)], axis=0).astype(jnp.bfloat16)
        sums = jnp.dot(parts, ones[...], preferred_element_type=jnp.float32)
        score = sums[0:8] + sums[8:16] + sums[16:24]
        logit = scale_v * score + bias_v
        tags = qbuf[k, pl.ds(q_rows, 16), :].astype(jnp.float32)
        block = jnp.concatenate([tags[0:1], tags[1:2]], axis=1)
        page = jnp.concatenate([tags[2:3], tags[3:4]], axis=1)
        positive = (block == me.astype(jnp.float32)) & (page == parity.astype(jnp.float32))
        sign = jnp.where(positive, 1.0, -1.0)
        t = -sign * logit
        decay = jnp.exp(-jnp.abs(t))
        lvec[...] += jnp.maximum(t, 0.0) + jnp.log1p(decay)
        slope = -sign * scale_v * jnp.where(t >= 0, 1.0, decay) / (1.0 + decay)
        return slope / total

    def backward(k, factor):
        q = qbuf[k, pl.ds(0, q_rows), :]
        grad_q = jnp.zeros((EMB, q_rows), jnp.float32)
        for c in range(3):
            coef = (xs[c] * factor[None]).reshape(chunk, q_rows).astype(jnp.bfloat16)
            grad_q = grad_q + jnp.dot(pgt[c], coef, preferred_element_type=jnp.float32)
            part = jnp.dot(coef, q, preferred_element_type=jnp.float32)
            rows = min(chunk, p_rows - c * chunk)
            here = pl.ds(c * chunk, rows)

            @pl.when(k == 0)
            def _():
                gp2[here, :] = part[:rows]

            @pl.when(k > 0)
            def _():
                gp2[here, :] += part[:rows]
        return grad_q

    def l_copy(stage, slot, offset):
        return pltpu.make_async_remote_copy(
            lsend.at[stage], (l1, l2)[stage].at[slot], l_send.at[stage], l_recv.at[stage],
            device_id=(peer(offset),), device_id_type=MESH,
        )

    def l_wait(stage, group, sem):
        buf = (l1, l2)[stage].at[pl.ds(1, len(group))]
        pltpu.make_async_copy(buf, buf, sem.at[stage]).wait()

    def tree(v):
        while v.shape[0] > 1:
            half = v.shape[0] // 2
            v = v[:half] + v[half:]
        return v[0]

    def g_copy(k):
        target = me
        for slot in range(1, 5):
            target = target + jnp.where(k == slot, flip[bits[slot - 1]], 0)
        return pltpu.make_async_remote_copy(
            gsend.at[k], grecv.at[k], g_send.at[k], g_recv.at[k], device_id=(target,), device_id_type=MESH,
        )

    def step(k, _):
        @pl.when(k > 0)
        def _():
            pltpu.make_async_copy(qbuf.at[k], qbuf.at[k], q_recv.at[k]).wait()

        factor = forward(k)

        @pl.when(k == 4)
        def _():
            v = jnp.sum(lvec[...], axis=0, keepdims=True)
            v = v[:, :EMB] + v[:, EMB:]
            lsend[0] = v
            l1[0] = v
            for slot, d in enumerate(group_a, 1):
                l_copy(0, slot, d).start()

        grad_q = backward(k, factor)

        @pl.when(k == 0)
        def _():
            gown[...] = grad_q

        @pl.when(k > 0)
        def _():
            gsend[k] = grad_q.astype(jnp.bfloat16)
            g_copy(k).start()

        return 0

    lax.fori_loop(0, 5, step, 0)

    l_wait(0, group_a, l_recv)
    v = tree(l1[...])
    if group_b:
        lsend[1] = v
        l2[0] = v
        for slot, d in enumerate(group_b, 1):
            l_copy(1, slot, d).start()
    grad = gown[...]
    for slot in range(1, 5):
        pltpu.make_async_copy(grecv.at[slot], grecv.at[slot], g_recv.at[slot]).wait()
        grad = grad + grecv[slot].astype(jnp.float32)
    gq_out[...] = grad.T
    if group_b:
        l_wait(1, group_b, l_recv)
        v = tree(l2[...])
    loss_out[0, 0] = jnp.sum(v) * (1.0 / (4 * QT))

    l_wait(0, group_a, l_send)
    if group_b:
        l_wait(1, group_b, l_send)
    for slot in range(1, 5):
        q_copies[slot].wait_send()
        pltpu.make_async_copy(gsend.at[slot], gsend.at[slot], g_send.at[slot]).wait()


def per_device(n_dev, queries, pages, counts, labels, logit_scale, logit_bias):
    n_query, q_tok, emb = queries.shape
    n_page, page_len, _ = pages.shape
    q_rows = n_query * q_tok
    p_rows = n_page * page_len
    p_pad = (p_rows + 47) // 48 * 48
    low = max(1, n_dev // 16)
    vmem = pl.BlockSpec(memory_space=pltpu.VMEM)
    smem = pl.BlockSpec(memory_space=pltpu.SMEM)
    bf16, f32 = jnp.bfloat16, jnp.float32
    loss, grad_q, grad_p = pl.pallas_call(
        lambda *refs: kernel(n_dev, q_rows, p_rows, *refs),
        out_shape=(
            jax.ShapeDtypeStruct((1, 1), f32),
            jax.ShapeDtypeStruct((q_rows, emb), f32),
            jax.ShapeDtypeStruct((page_len, n_page, emb), f32),
        ),
        in_specs=[pl.BlockSpec(memory_space=pltpu.HBM)] * 2 + [smem] * 4,
        out_specs=(smem, vmem, vmem),
        scratch_shapes=[
            pltpu.VMEM((5, q_rows + 16, emb), bf16),
            pltpu.VMEM((p_pad, emb), bf16),
            pltpu.VMEM((3, emb, p_pad // 3), bf16),
            pltpu.VMEM((3, p_pad // 24, 8, q_rows), f32),
            pltpu.VMEM((emb, q_rows), f32),
            pltpu.VMEM((5, emb, q_rows), bf16),
            pltpu.VMEM((5, emb, q_rows), bf16),
            pltpu.VMEM((q_rows, q_rows), bf16),
            pltpu.VMEM((8, q_rows), f32),
            pltpu.VMEM((2, 1, emb), f32),
            pltpu.VMEM((16, 1, emb), f32),
            pltpu.VMEM((low, 1, emb), f32),
            pltpu.SemaphoreType.DMA((2,)),
            pltpu.SemaphoreType.DMA((5,)),
            pltpu.SemaphoreType.DMA((5,)),
            pltpu.SemaphoreType.DMA((5,)),
            pltpu.SemaphoreType.DMA((5,)),
            pltpu.SemaphoreType.DMA((2,)),
            pltpu.SemaphoreType.DMA((2,)),
        ],
        compiler_params=pltpu.CompilerParams(
            collective_id=0, has_side_effects=True, vmem_limit_bytes=32 * 1024 * 1024
        ),
    )(
        queries.reshape(q_rows, emb),
        jnp.transpose(pages, (1, 0, 2)),
        counts,
        labels,
        logit_scale.reshape(1),
        logit_bias.reshape(1),
    )
    return loss.reshape(()), grad_q.reshape(n_query, q_tok, emb), jnp.transpose(grad_p, (1, 0, 2))


def solution(mesh):
    n_dev = mesh.shape["dp"]
    placed = (P("dp", None, None), P("dp", None, None), P("dp"), P("dp"), P(), P())
    return jax.shard_map(
        lambda *args: per_device(n_dev, *args),
        mesh=mesh,
        in_specs=placed,
        out_specs=(P(), P("dp", None, None), P("dp", None, None)),
        check_vma=False,
    )
```

```python
import jax
import jax.numpy as jnp
from jax import lax
from jax.experimental import pallas as pl
from jax.experimental.pallas import tpu as pltpu
from jax.sharding import PartitionSpec as P

EMB = 128
QT = 32
TAU = 0.1
EXP2_SCALE = 1.4426950408889634 / TAU
MIN_COUNT = 700
CHUNKS = 3
MESH = pl.DeviceIdType.MESH


def combos(bits):
    return [sum(1 << b for i, b in enumerate(bits) if s >> i & 1) for s in range(1 << len(bits))]


def far_first(offsets, far):
    return sorted(range(1, len(offsets)), key=lambda s: (-sum(far[b] for b in range(8) if offsets[s] >> b & 1), s))


def kernel(
    n_dev, q_rows, p_rows,
    q_hbm, p_hbm, counts_hbm, labels_hbm, scale_hbm, bias_hbm,
    loss_out, gq_out, gp_out,
    counts, labels, scale, bias,
    qbuf, tags, pg, pgt, xs, tops, totals, factors, gown, gsend, grecv, ones, lsend, l1, l2,
    local_sem, q_send, q_recv, t_send, t_recv, g_send, g_recv, l_send, l_recv,
):
    me = lax.axis_index("dp")
    n_bits = n_dev.bit_length() - 1
    flip = [(1 << b) - 2 * (1 << b) * ((me // (1 << b)) % 2) for b in range(n_bits)]

    def peer(offset):
        out = me
        for b in range(n_bits):
            if offset >> b & 1:
                out = out + flip[b]
        return out

    bits = [n_bits - 2, n_bits - 1, n_bits - 4, n_bits - 3]
    if n_dev == 256:
        groups = [combos([0, 3, 4, 5]), combos([1, 2, 6, 7])]
        far = [0.5, 1, 2, 1, 2, 4, 1, 2]
    else:
        groups = [combos(range(2)), combos(range(2, n_bits))]
        far = [1] * 8
    order = [far_first(g, far) for g in groups]
    p_pad = pg.shape[0]
    chunk = p_pad // CHUNKS

    barrier = pltpu.get_barrier_semaphore()

    def greet(offset):
        pl.semaphore_signal(barrier, inc=1, device_id=(peer(offset),), device_id_type=MESH)

    first = [1 << bits[slot - 1] for slot in (4, 3, 2, 1)]
    others = [g[s] for g, o in zip(groups, order) for s in o if g[s] not in first]
    for d in first:
        greet(d)

    pg[pl.ds(p_pad - 16, 16), :] = jnp.zeros((16, EMB), jnp.bfloat16)
    local = [
        pltpu.make_async_copy(src, dst, local_sem.at[i])
        for i, (src, dst) in enumerate(
            [
                (labels_hbm, labels),
                (q_hbm, qbuf.at[0]),
                (p_hbm.reshape(p_rows, EMB), pg.at[pl.ds(0, p_rows)]),
                (counts_hbm, counts),
                (scale_hbm, scale),
                (bias_hbm, bias),
            ]
        )
    ]
    for copy in local:
        copy.start()
    for d in others:
        greet(d)

    local[0].wait()
    row = lax.broadcasted_iota(jnp.int32, (16, EMB), 0)
    lane = lax.broadcasted_iota(jnp.int32, (16, EMB), 1)
    which = (row & 1) * (EMB // QT) + lane // QT
    label = jnp.zeros((16, EMB), jnp.int32)
    for q in range(q_rows // QT):
        label = jnp.where(which == q, labels[q], label)
    tags[0] = jnp.where(row < 2, label >> 1, label & 1).astype(jnp.float32).astype(jnp.bfloat16)

    pl.semaphore_wait(barrier, len(first) + len(others))

    def q_copy(slot):
        return pltpu.make_async_remote_copy(
            q_hbm, qbuf.at[slot], q_send.at[slot], q_recv.at[slot],
            device_id=(peer(1 << bits[slot - 1]),), device_id_type=MESH,
        )

    def t_copy(slot):
        return pltpu.make_async_remote_copy(
            tags.at[0], tags.at[slot], t_send.at[slot], t_recv.at[slot],
            device_id=(peer(1 << bits[slot - 1]),), device_id_type=MESH,
        )

    for slot in (4, 3, 2, 1):
        q_copy(slot).start()
    for slot in (4, 3, 2, 1):
        t_copy(slot).start()

    group_row = lax.broadcasted_iota(jnp.int32, (q_rows, q_rows), 0) // QT
    group_col = lax.broadcasted_iota(jnp.int32, (q_rows, q_rows), 1) // QT
    ones[...] = jnp.where(group_row == group_col, 1.0, 0.0).astype(jnp.bfloat16)
    gp2 = gp_out.reshape(p_rows, EMB)
    sub = lax.broadcasted_iota(jnp.int32, (8, q_rows), 0)
    parity = sub & 1
    for copy in local[1:]:
        copy.wait()
    limit = 2 * jnp.where(parity == 0, counts[0], counts[1]) - sub

    for c in range(CHUNKS):
        pgt[c] = pg[pl.ds(c * chunk, chunk), :].astype(jnp.float32).T.astype(jnp.bfloat16)

    def all_rows(vec, op):
        vec = op(vec, pltpu.roll(vec, 2, 0))
        return op(vec, pltpu.roll(vec, 4, 0))

    def forward(k, _):
        @pl.when(k > 0)
        def _():
            pltpu.make_async_copy(qbuf.at[k], qbuf.at[k], q_recv.at[k]).wait()

        q = qbuf[k]
        top = jnp.full((8, q_rows), -jnp.inf, jnp.float32)
        for c in range(CHUNKS):
            x = lax.dot_general(
                pg[pl.ds(c * chunk, chunk), :], q, (((1,), (1,)), ((), ())), preferred_element_type=jnp.float32
            ).reshape(chunk // 8, 8, q_rows)
            if (c + 1) * chunk > 2 * MIN_COUNT:
                start = c * chunk + 8 * lax.broadcasted_iota(jnp.int32, x.shape, 0)
                x = jnp.where(limit[None] > start, x, -jnp.inf)
            xs[k, c] = x
            top = jnp.maximum(top, jnp.max(x, axis=0))
        top = all_rows(top, jnp.maximum)
        tops[k] = top
        total = jnp.zeros((8, q_rows), jnp.float32)
        for c in range(CHUNKS):
            e = jnp.exp2((xs[k, c] - top[None]) * EXP2_SCALE)
            xs[k, c] = e
            total = total + jnp.sum(e, axis=0)
        totals[k] = total
        return 0

    lax.fori_loop(0, 5, forward, 0)

    for slot in range(1, 5):
        t_copy(slot).wait_recv()
    parts = []
    total = [all_rows(totals[k], jnp.add) for k in range(5)]
    for k in range(5):
        soft = tops[k] + TAU * jnp.log(total[k])
        hi = soft.astype(jnp.bfloat16).astype(jnp.float32)
        rest = soft - hi
        mid = rest.astype(jnp.bfloat16).astype(jnp.float32)
        parts += [hi, mid, rest - mid]
    parts = jnp.concatenate(parts + [jnp.zeros_like(parts[0])], axis=0).astype(jnp.bfloat16)
    sums = jnp.dot(parts, ones[...], preferred_element_type=jnp.float32).reshape(16, 8, q_rows)
    loss = jnp.zeros((8, q_rows), jnp.float32)
    for k in range(5):
        score = sums[3 * k] + sums[3 * k + 1] + sums[3 * k + 2]
        logit = scale[0] * score + bias[0]
        tag = tags[k].astype(jnp.float32)
        block = jnp.concatenate([tag[0:1], tag[1:2]], axis=1)
        page = jnp.concatenate([tag[2:3], tag[3:4]], axis=1)
        positive = (block == me.astype(jnp.float32)) & (page == parity.astype(jnp.float32))
        sign = jnp.where(positive, 1.0, -1.0)
        t = -sign * logit
        decay = jnp.exp(-jnp.abs(t))
        loss = loss + (jnp.maximum(t, 0.0) + jnp.log1p(decay))
        slope = -sign * scale[0] * jnp.where(t >= 0, 1.0, decay) / (1.0 + decay)
        factors[k] = slope / total[k]

    def l_copy(stage, slot):
        return pltpu.make_async_remote_copy(
            lsend.at[stage], (l1, l2)[stage].at[slot], l_send.at[stage], l_recv.at[stage],
            device_id=(peer(groups[stage][slot]),), device_id_type=MESH,
        )

    def l_wait(stage, sem):
        buf = (l1, l2)[stage].at[pl.ds(1, len(groups[stage]) - 1)]
        pltpu.make_async_copy(buf, buf, sem.at[stage]).wait()

    def l_start(stage, v):
        lsend[stage] = v
        (l1, l2)[stage][0] = v
        for slot in order[stage]:
            l_copy(stage, slot).start()

    def tree(v):
        while v.shape[0] > 1:
            half = v.shape[0] // 2
            v = v[:half] + v[half:]
        return v[0]

    loss = jnp.sum(loss, axis=0, keepdims=True)
    l_start(0, loss[:, :EMB] + loss[:, EMB:])

    def backward(step, _):
        k = 4 - step
        q = qbuf[k]
        factor = factors[k]
        grad_q = jnp.zeros((EMB, q_rows), jnp.float32)
        for c in range(CHUNKS):
            coef = (xs[k, c] * factor[None]).reshape(chunk, q_rows).astype(jnp.bfloat16)
            grad_q = grad_q + jnp.dot(pgt[c], coef, preferred_element_type=jnp.float32)
            part = jnp.dot(coef, q, preferred_element_type=jnp.float32)
            rows = min(chunk, p_rows - c * chunk)
            here = pl.ds(c * chunk, rows)

            @pl.when(step == 0)
            def _():
                gp2[here, :] = part[:rows]

            @pl.when(step > 0)
            def _():
                gp2[here, :] += part[:rows]

        @pl.when(k == 0)
        def _():
            gown[...] = grad_q

        @pl.when(k > 0)
        def _():
            gsend[k] = grad_q.astype(jnp.bfloat16)
            target = me
            for slot in range(1, 5):
                target = target + jnp.where(k == slot, flip[bits[slot - 1]], 0)
            pltpu.make_async_remote_copy(
                gsend.at[k], grecv.at[k], g_send.at[k], g_recv.at[k], device_id=(target,), device_id_type=MESH,
            ).start()

        return 0

    lax.fori_loop(0, 5, backward, 0)

    l_wait(0, l_recv)
    l_start(1, tree(l1[...]))
    grad = gown[...]
    for slot in (1, 2, 3, 4):
        pltpu.make_async_copy(grecv.at[slot], grecv.at[slot], g_recv.at[slot]).wait()
        grad = grad + grecv[slot].astype(jnp.float32)
    gq_out[...] = grad.T
    for slot in range(1, 5):
        q_copy(slot).wait_send()
        t_copy(slot).wait_send()
        pltpu.make_async_copy(gsend.at[slot], gsend.at[slot], g_send.at[slot]).wait()
    l_wait(0, l_send)
    l_wait(1, l_recv)
    loss_out[...] = tree(l2[...])
    l_wait(1, l_send)


def finish(loss, gq, gp, loss_out, gq_out, gp_out, sem):
    copies = [pltpu.make_async_copy(gp, gp_out, sem.at[0]), pltpu.make_async_copy(gq, gq_out, sem.at[1])]
    for copy in copies:
        copy.start()
    loss_out[0, 0] = jnp.sum(loss[...]) * (1.0 / (4 * QT))
    for copy in copies:
        copy.wait()


def per_device(n_dev, queries, pages, counts, labels, logit_scale, logit_bias):
    n_query, q_tok, emb = queries.shape
    n_page, page_len, _ = pages.shape
    q_rows = n_query * q_tok
    p_rows = n_page * page_len
    p_pad = (p_rows + 16 * CHUNKS - 1) // (16 * CHUNKS) * (16 * CHUNKS)
    n2 = 16 if n_dev == 256 else max(2, n_dev // 4)
    vmem = pl.BlockSpec(memory_space=pltpu.VMEM)
    smem = pl.BlockSpec(memory_space=pltpu.SMEM)
    hbm = pl.BlockSpec(memory_space=pltpu.HBM)
    bf16, f32 = jnp.bfloat16, jnp.float32
    dma = pltpu.SemaphoreType.DMA
    gp_shape = jax.ShapeDtypeStruct((page_len, n_page, emb), f32)
    gq_shape = jax.ShapeDtypeStruct((q_rows, emb), f32)
    operands = (
        queries.reshape(q_rows, emb),
        jnp.transpose(pages, (1, 0, 2)),
        counts,
        labels,
        logit_scale.reshape(1),
        logit_bias.reshape(1),
    )
    parts = pl.pallas_call(
        lambda *refs: kernel(n_dev, q_rows, p_rows, *refs),
        out_shape=(jax.ShapeDtypeStruct((1, emb), f32), gq_shape, gp_shape),
        in_specs=[hbm] * 6,
        out_specs=(vmem, vmem, vmem),
        scratch_shapes=[
            pltpu.SMEM(counts.shape, jnp.int32),
            pltpu.SMEM(labels.shape, jnp.int32),
            pltpu.SMEM((1,), f32),
            pltpu.SMEM((1,), f32),
            pltpu.VMEM((5, q_rows, emb), bf16),
            pltpu.VMEM((5, 16, emb), bf16),
            pltpu.VMEM((p_pad, emb), bf16),
            pltpu.VMEM((CHUNKS, emb, p_pad // CHUNKS), bf16),
            pltpu.VMEM((5, CHUNKS, p_pad // (8 * CHUNKS), 8, q_rows), f32),
            pltpu.VMEM((5, 8, q_rows), f32),
            pltpu.VMEM((5, 8, q_rows), f32),
            pltpu.VMEM((5, 8, q_rows), f32),
            pltpu.VMEM((emb, q_rows), f32),
            pltpu.VMEM((5, emb, q_rows), bf16),
            pltpu.VMEM((5, emb, q_rows), bf16),
            pltpu.VMEM((q_rows, q_rows), bf16),
            pltpu.VMEM((2, 1, emb), f32),
            pltpu.VMEM((n_dev // n2, 1, emb), f32),
            pltpu.VMEM((n2, 1, emb), f32),
            dma((6,)),
            dma((5,)),
            dma((5,)),
            dma((5,)),
            dma((5,)),
            dma((5,)),
            dma((5,)),
            dma((2,)),
            dma((2,)),
        ],
        compiler_params=pltpu.CompilerParams(
            collective_id=0, has_side_effects=True, vmem_limit_bytes=40 * 1024 * 1024
        ),
    )(*[pltpu.with_memory_space_constraint(x, pltpu.HBM) for x in operands[:4]], *operands[4:])
    loss, grad_q, grad_p = pl.pallas_call(
        finish,
        out_shape=(jax.ShapeDtypeStruct((1, 1), f32), gq_shape, gp_shape),
        in_specs=[vmem] * 3,
        out_specs=(smem, hbm, hbm),
        scratch_shapes=[dma((2,))],
        compiler_params=pltpu.CompilerParams(vmem_limit_bytes=16 * 1024 * 1024),
    )(*parts)
    return loss.reshape(()), grad_q.reshape(n_query, q_tok, emb), jnp.transpose(grad_p, (1, 0, 2))


def solution(mesh):
    n_dev = mesh.shape["dp"]
    placed = (P("dp", None, None), P("dp", None, None), P("dp"), P("dp"), P(), P())
    return jax.shard_map(
        lambda *args: per_device(n_dev, *args),
        mesh=mesh,
        in_specs=placed,
        out_specs=(P(), P("dp", None, None), P("dp", None, None)),
        check_vma=False,
    )
```

```python
import jax
import jax.numpy as jnp
from jax import lax
from jax.experimental import pallas as pl
from jax.experimental.pallas import tpu as pltpu
from jax.sharding import PartitionSpec as P

EMB = 128
QT = 32
TAU = 0.1
EXP2_SCALE = 1.4426950408889634 / TAU
MIN_COUNT = 700
CHUNKS = 3
PIECES = 4
MESH = pl.DeviceIdType.MESH


def combos(bits):
    return [sum(1 << b for i, b in enumerate(bits) if s >> i & 1) for s in range(1 << len(bits))]


def far_first(offsets, far):
    return sorted(range(1, len(offsets)), key=lambda s: (-sum(far[b] for b in range(8) if offsets[s] >> b & 1), s))


def loss_groups(n_bits):
    first = [1, 2, 6, 7] if n_bits == 8 else list(range(n_bits // 2))
    return [combos(first), combos([b for b in range(n_bits) if b not in first])]


def kernel(
    n_dev, q_rows, p_rows,
    q_hbm, p_hbm, counts_hbm, labels_hbm, scale_hbm, bias_hbm,
    loss_out, gq_out, gp_out,
    counts, labels, scale, bias,
    qbuf, pg, pgt, xs, tops, totals, factors, gown, gsend, grecv, ones, lsend, l1, l2,
    local_sem, q_send, q_recv, g_send, g_recv, l_send, l_recv,
):
    me = lax.axis_index("dp")
    n_bits = n_dev.bit_length() - 1
    flip = [(1 << b) - 2 * (1 << b) * ((me // (1 << b)) % 2) for b in range(n_bits)]

    def peer(offset):
        out = me
        for b in range(n_bits):
            if offset >> b & 1:
                out = out + flip[b]
        return out

    bits = [n_bits - 2, n_bits - 1, n_bits - 3, n_bits - 4]
    groups = loss_groups(n_bits)
    far = [0.5, 1, 2, 1, 2, 4, 1, 2]
    lbufs = (l1, l2)
    order = [far_first(g, far) for g in groups]
    p_pad = pg.shape[0]
    chunk = p_pad // CHUNKS

    barrier = pltpu.get_barrier_semaphore()

    def greet(offset):
        pl.semaphore_signal(barrier, inc=1, device_id=(peer(offset),), device_id_type=MESH)

    first = [1 << bits[slot - 1] for slot in (3, 4, 2, 1)]
    others = [groups[i][order[i][n]] for n in range(len(order[0])) for i in (0, 1) if n < len(order[i])]
    others = [d for d in others if d not in first]
    for d in first:
        greet(d)

    pg[pl.ds(p_pad - 16, 16), :] = jnp.zeros((16, EMB), jnp.bfloat16)
    local = [
        pltpu.make_async_copy(src, dst, local_sem.at[i])
        for i, (src, dst) in enumerate(
            [
                (labels_hbm, labels),
                (q_hbm, qbuf.at[0, pl.ds(0, q_rows)]),
                (p_hbm.reshape(p_rows, EMB), pg.at[pl.ds(0, p_rows)]),
                (counts_hbm, counts),
                (scale_hbm, scale),
                (bias_hbm, bias),
            ]
        )
    ]
    for d in others:
        greet(d)
    for copy in local:
        copy.start()

    local[0].wait()
    row = lax.broadcasted_iota(jnp.int32, (16, EMB), 0)
    lane = lax.broadcasted_iota(jnp.int32, (16, EMB), 1)
    which = (row & 1) * (EMB // QT) + lane // QT
    label = jnp.zeros((16, EMB), jnp.int32)
    for q in range(q_rows // QT):
        label = jnp.where(which == q, labels[q], label)
    qbuf[0, pl.ds(q_rows, 16), :] = jnp.where(row < 2, label >> 1, label & 1).astype(jnp.float32).astype(jnp.bfloat16)

    local[1].wait()
    pl.semaphore_wait(barrier, len(first) + len(others))

    def q_copy(slot):
        return pltpu.make_async_remote_copy(
            qbuf.at[0], qbuf.at[slot], q_send.at[slot], q_recv.at[slot],
            device_id=(peer(1 << bits[slot - 1]),), device_id_type=MESH,
        )

    for slot in (3, 4, 2, 1):
        q_copy(slot).start()

    group_row = lax.broadcasted_iota(jnp.int32, (q_rows, q_rows), 0) // QT
    group_col = lax.broadcasted_iota(jnp.int32, (q_rows, q_rows), 1) // QT
    ones[...] = jnp.where(group_row == group_col, 1.0, 0.0).astype(jnp.bfloat16)
    sub = lax.broadcasted_iota(jnp.int32, (8, q_rows), 0)
    parity = sub & 1
    for copy in local[2:]:
        copy.wait()
    limit = 2 * jnp.where(parity == 0, counts[0], counts[1]) - sub

    for c in range(CHUNKS):
        pgt[c] = pg[pl.ds(c * chunk, chunk), :].astype(jnp.float32).T.astype(jnp.bfloat16)

    gp_out[...] = jnp.zeros_like(gp_out)

    def all_rows(vec, op):
        vec = op(vec, pltpu.roll(vec, 2, 0))
        return op(vec, pltpu.roll(vec, 4, 0))

    def forward(k, _):
        @pl.when(k > 0)
        def _():
            pltpu.make_async_copy(qbuf.at[k], qbuf.at[k], q_recv.at[k]).wait()

        q = qbuf[k, pl.ds(0, q_rows), :]
        top = jnp.full((8, q_rows), -jnp.inf, jnp.float32)
        for c in range(CHUNKS):
            x = lax.dot_general(
                pg[pl.ds(c * chunk, chunk), :], q, (((1,), (1,)), ((), ())), preferred_element_type=jnp.float32
            ).reshape(chunk // 8, 8, q_rows)
            if (c + 1) * chunk > 2 * MIN_COUNT:
                start = c * chunk + 8 * lax.broadcasted_iota(jnp.int32, x.shape, 0)
                x = jnp.where(limit[None] > start, x, -jnp.inf)
            xs[k, c] = x
            top = jnp.maximum(top, jnp.max(x, axis=0))
        top = all_rows(top, jnp.maximum)
        tops[k] = top
        total = jnp.zeros((8, q_rows), jnp.float32)
        for c in range(CHUNKS):
            e = jnp.exp2((xs[k, c] - top[None]) * EXP2_SCALE)
            xs[k, c] = e
            total = total + jnp.sum(e, axis=0)
        totals[k] = total

        return 0

    lax.fori_loop(0, 5, forward, 0)

    parts = []
    total = [all_rows(totals[k], jnp.add) for k in range(5)]
    for k in range(5):
        soft = tops[k] + TAU * jnp.log(total[k])
        hi = soft.astype(jnp.bfloat16).astype(jnp.float32)
        rest = soft - hi
        mid = rest.astype(jnp.bfloat16).astype(jnp.float32)
        parts += [hi, mid, rest - mid]
    parts = jnp.concatenate(parts + [jnp.zeros_like(parts[0])], axis=0).astype(jnp.bfloat16)
    sums = jnp.dot(parts, ones[...], preferred_element_type=jnp.float32).reshape(16, 8, q_rows)
    loss = jnp.zeros((8, q_rows), jnp.float32)
    for k in range(5):
        score = sums[3 * k] + sums[3 * k + 1] + sums[3 * k + 2]
        logit = scale[0] * score + bias[0]
        tag = qbuf[k, pl.ds(q_rows, 16), :].astype(jnp.float32)
        block = jnp.concatenate([tag[0:1], tag[1:2]], axis=1)
        page = jnp.concatenate([tag[2:3], tag[3:4]], axis=1)
        positive = (block == me.astype(jnp.float32)) & (page == parity.astype(jnp.float32))
        sign = jnp.where(positive, 1.0, -1.0)
        t = -sign * logit
        decay = jnp.exp(-jnp.abs(t))
        loss = loss + (jnp.maximum(t, 0.0) + jnp.log1p(decay))
        slope = -sign * scale[0] * jnp.where(t >= 0, 1.0, decay) / (1.0 + decay)
        factors[k] = slope / total[k]

    def l_copy(stage, slot):
        return pltpu.make_async_remote_copy(
            lsend.at[stage], lbufs[stage].at[slot], l_send.at[stage], l_recv.at[stage],
            device_id=(peer(groups[stage][slot]),), device_id_type=MESH,
        )

    def l_wait(stage, sem):
        buf = lbufs[stage].at[pl.ds(1, len(groups[stage]) - 1)]
        pltpu.make_async_copy(buf, buf, sem.at[stage]).wait()

    def l_start(stage, v):
        lsend[stage] = v
        lbufs[stage][0] = v
        for slot in order[stage]:
            l_copy(stage, slot).start()

    def tree(v):
        while v.shape[0] > 1:
            half = v.shape[0] // 2
            v = v[:half] + v[half:]
        return v[0]

    loss = jnp.sum(loss, axis=0, keepdims=True)
    l_start(0, loss[:, :EMB] + loss[:, EMB:])

    def backward(step, _):
        k = 4 - step
        q = qbuf[k, pl.ds(0, q_rows), :]
        factor = factors[k]
        grad_q = jnp.zeros((EMB, q_rows), jnp.float32)
        for c in range(CHUNKS):
            coef = (xs[k, c] * factor[None]).reshape(chunk, q_rows).astype(jnp.bfloat16)
            grad_q = grad_q + jnp.dot(pgt[c], coef, preferred_element_type=jnp.float32)
            part = jnp.dot(coef, q, preferred_element_type=jnp.float32)
            here = pl.ds(c * chunk, chunk)

            gp_out[here, :] += part

        @pl.when(k == 0)
        def _():
            gown[...] = grad_q

        @pl.when(k > 0)
        def _():
            gsend[k] = grad_q.astype(jnp.bfloat16)
            target = me
            for slot in range(1, 5):
                target = target + jnp.where(k == slot, flip[bits[slot - 1]], 0)
            pltpu.make_async_remote_copy(
                gsend.at[k], grecv.at[k], g_send.at[k], g_recv.at[k], device_id=(target,), device_id_type=MESH,
            ).start()

        return 0

    lax.fori_loop(0, 5, backward, 0)

    l_wait(0, l_recv)
    l_start(1, tree(l1[...]))
    grad = gown[...]
    for slot in (1, 2, 3, 4):
        pltpu.make_async_copy(grecv.at[slot], grecv.at[slot], g_recv.at[slot]).wait()
        grad = grad + grecv[slot].astype(jnp.float32)
    gq_out[...] = grad.T
    for slot in range(1, 5):
        q_copy(slot).wait_send()
        pltpu.make_async_copy(gsend.at[slot], gsend.at[slot], g_send.at[slot]).wait()
    l_wait(0, l_send)
    l_wait(1, l_recv)
    loss_out[...] = tree(l2[...])
    l_wait(1, l_send)


def finish(loss, gq, gp, loss_out, gq_out, gp_out, sem):
    n_page, emb = gp_out.shape[1:]
    rows = gp_out.shape[0] * n_page
    flat = gp_out.reshape(rows, emb)
    step = (rows // PIECES + 7) // 8 * 8
    copies = [pltpu.make_async_copy(gq, gq_out, sem.at[PIECES])]
    for i in range(PIECES):
        part = pl.ds(i * step, min(step, rows - i * step))
        copies.append(pltpu.make_async_copy(gp.at[part], flat.at[part], sem.at[i]))
    for copy in copies:
        copy.start()
    loss_out[0, 0] = jnp.sum(loss[...]) * (1.0 / (4 * QT))
    for copy in copies:
        copy.wait()


def per_device(n_dev, queries, pages, counts, labels, logit_scale, logit_bias):
    n_query, q_tok, emb = queries.shape
    n_page, page_len, _ = pages.shape
    q_rows = n_query * q_tok
    p_rows = n_page * page_len
    p_pad = (p_rows + 16 * CHUNKS - 1) // (16 * CHUNKS) * (16 * CHUNKS)
    sizes = [len(g) for g in loss_groups(n_dev.bit_length() - 1)]
    vmem = pl.BlockSpec(memory_space=pltpu.VMEM)
    smem = pl.BlockSpec(memory_space=pltpu.SMEM)
    hbm = pl.BlockSpec(memory_space=pltpu.HBM)
    bf16, f32 = jnp.bfloat16, jnp.float32
    dma = pltpu.SemaphoreType.DMA
    gp_shape = jax.ShapeDtypeStruct((page_len, n_page, emb), f32)
    gq_shape = jax.ShapeDtypeStruct((q_rows, emb), f32)
    operands = (
        queries.reshape(q_rows, emb),
        jnp.transpose(pages, (1, 0, 2)),
        counts,
        labels,
        logit_scale.reshape(1),
        logit_bias.reshape(1),
    )
    parts = pl.pallas_call(
        lambda *refs: kernel(n_dev, q_rows, p_rows, *refs),
        out_shape=(jax.ShapeDtypeStruct((1, emb), f32), gq_shape, jax.ShapeDtypeStruct((p_pad, emb), f32)),
        in_specs=[hbm] * 6,
        out_specs=(vmem, vmem, vmem),
        scratch_shapes=[
            pltpu.SMEM(counts.shape, jnp.int32),
            pltpu.SMEM(labels.shape, jnp.int32),
            pltpu.SMEM((1,), f32),
            pltpu.SMEM((1,), f32),
            pltpu.VMEM((5, q_rows + 16, emb), bf16),
            pltpu.VMEM((p_pad, emb), bf16),
            pltpu.VMEM((CHUNKS, emb, p_pad // CHUNKS), bf16),
            pltpu.VMEM((5, CHUNKS, p_pad // (8 * CHUNKS), 8, q_rows), f32),
            pltpu.VMEM((5, 8, q_rows), f32),
            pltpu.VMEM((5, 8, q_rows), f32),
            pltpu.VMEM((5, 8, q_rows), f32),
            pltpu.VMEM((emb, q_rows), f32),
            pltpu.VMEM((5, emb, q_rows), bf16),
            pltpu.VMEM((5, emb, q_rows), bf16),
            pltpu.VMEM((q_rows, q_rows), bf16),
            pltpu.VMEM((2, 1, emb), f32),
            *[pltpu.VMEM((n, 1, emb), f32) for n in sizes],
            dma((6,)),
            dma((5,)),
            dma((5,)),
            dma((5,)),
            dma((5,)),
            dma((2,)),
            dma((2,)),
        ],
        compiler_params=pltpu.CompilerParams(
            collective_id=0, has_side_effects=True, vmem_limit_bytes=40 * 1024 * 1024
        ),
    )(*[pltpu.with_memory_space_constraint(x, pltpu.HBM) for x in operands[:4]], *operands[4:])
    loss, grad_q, grad_p = pl.pallas_call(
        finish,
        out_shape=(jax.ShapeDtypeStruct((1, 1), f32), gq_shape, gp_shape),
        in_specs=[vmem] * 3,
        out_specs=(smem, hbm, hbm),
        scratch_shapes=[dma((PIECES + 1,))],
        compiler_params=pltpu.CompilerParams(vmem_limit_bytes=16 * 1024 * 1024),
    )(*parts)
    return loss.reshape(()), grad_q.reshape(n_query, q_tok, emb), jnp.transpose(grad_p, (1, 0, 2))


def solution(mesh):
    n_dev = mesh.shape["dp"]
    placed = (P("dp", None, None), P("dp", None, None), P("dp"), P("dp"), P(), P())
    return jax.shard_map(
        lambda *args: per_device(n_dev, *args),
        mesh=mesh,
        in_specs=placed,
        out_specs=(P(), P("dp", None, None), P("dp", None, None)),
        check_vma=False,
    )
```

```python
import jax
import jax.numpy as jnp
from jax import lax
from jax.experimental import pallas as pl
from jax.experimental.pallas import tpu as pltpu
from jax.sharding import PartitionSpec as P

EMB = 128
QT = 32
TAU = 0.1
EXP2_SCALE = 1.4426950408889634 / TAU
MIN_COUNT = 700
CHUNKS = 3
MESH = pl.DeviceIdType.MESH


def combos(bits):
    return [sum(1 << b for i, b in enumerate(bits) if s >> i & 1) for s in range(1 << len(bits))]


def far_first(offsets, far):
    return sorted(range(1, len(offsets)), key=lambda s: (-sum(far[b] for b in range(8) if offsets[s] >> b & 1), s))


def loss_groups(n_bits):
    first = [0, 1, 2, 6, 7] if n_bits == 8 else list(range(n_bits // 2))
    return [combos(first), combos([b for b in range(n_bits) if b not in first])]


def kernel(
    n_dev, q_rows, p_rows,
    q_hbm, p_hbm, counts_hbm, labels_hbm, scale_hbm, bias_hbm,
    loss_out, gq_out, gp_out,
    counts, labels, scale, bias,
    qbuf, pg, pgt, xs, tops, totals, factors, gown, gsend, grecv, ones, lsend, l1, l2,
    local_sem, q_send, q_recv, g_send, g_recv, l_send, l_recv,
):
    me = lax.axis_index("dp")
    n_bits = n_dev.bit_length() - 1
    flip = [(1 << b) - 2 * (1 << b) * ((me // (1 << b)) % 2) for b in range(n_bits)]

    def peer(offset):
        out = me
        for b in range(n_bits):
            if offset >> b & 1:
                out = out + flip[b]
        return out

    bits = [n_bits - 2, n_bits - 1, n_bits - 3, n_bits - 4]
    groups = loss_groups(n_bits)
    far = [0.5, 1, 2, 1, 2, 4, 1, 2]
    lbufs = (l1, l2)
    order = [far_first(g, far) for g in groups]
    p_pad = pg.shape[0]
    chunk = p_pad // CHUNKS

    barrier = pltpu.get_barrier_semaphore()

    def greet(offset):
        pl.semaphore_signal(barrier, inc=1, device_id=(peer(offset),), device_id_type=MESH)

    first = [1 << bits[slot - 1] for slot in (3, 4, 2, 1)]
    others = [groups[i][order[i][n]] for n in range(31) for i in (0, 1) if n < len(order[i])]
    others = [d for d in others if d not in first]
    for d in first:
        greet(d)

    pg[pl.ds(p_pad - 16, 16), :] = jnp.zeros((16, EMB), jnp.bfloat16)
    local = [
        pltpu.make_async_copy(src, dst, local_sem.at[i])
        for i, (src, dst) in enumerate(
            [
                (labels_hbm, labels),
                (q_hbm, qbuf.at[0, pl.ds(0, q_rows)]),
                (p_hbm.reshape(p_rows, EMB), pg.at[pl.ds(0, p_rows)]),
                (counts_hbm, counts),
                (scale_hbm, scale),
                (bias_hbm, bias),
            ]
        )
    ]
    for d in others:
        greet(d)
    for copy in local:
        copy.start()

    local[0].wait()
    row = lax.broadcasted_iota(jnp.int32, (16, EMB), 0)
    lane = lax.broadcasted_iota(jnp.int32, (16, EMB), 1)
    which = (row & 1) * (EMB // QT) + lane // QT
    label = jnp.zeros((16, EMB), jnp.int32)
    for q in range(q_rows // QT):
        label = jnp.where(which == q, labels[q], label)
    qbuf[0, pl.ds(q_rows, 16), :] = jnp.where(row < 2, label >> 1, label & 1).astype(jnp.float32).astype(jnp.bfloat16)

    local[1].wait()
    pl.semaphore_wait(barrier, len(first) + len(others))

    def q_copy(slot):
        return pltpu.make_async_remote_copy(
            qbuf.at[0], qbuf.at[slot], q_send.at[slot], q_recv.at[slot],
            device_id=(peer(1 << bits[slot - 1]),), device_id_type=MESH,
        )

    for slot in (3, 4, 2, 1):
        q_copy(slot).start()

    group_row = lax.broadcasted_iota(jnp.int32, (q_rows, q_rows), 0) // QT
    group_col = lax.broadcasted_iota(jnp.int32, (q_rows, q_rows), 1) // QT
    ones[...] = jnp.where(group_row == group_col, 1.0, 0.0).astype(jnp.bfloat16)
    sub = lax.broadcasted_iota(jnp.int32, (8, q_rows), 0)
    parity = sub & 1
    for copy in local[2:]:
        copy.wait()
    limit = 2 * jnp.where(parity == 0, counts[0], counts[1]) - sub

    for c in range(CHUNKS):
        pgt[c] = pg[pl.ds(c * chunk, chunk), :].astype(jnp.float32).T.astype(jnp.bfloat16)

    gp_out[...] = jnp.zeros_like(gp_out)

    def all_rows(vec, op):
        vec = op(vec, pltpu.roll(vec, 2, 0))
        return op(vec, pltpu.roll(vec, 4, 0))

    def forward(k, _):
        @pl.when(k > 0)
        def _():
            pltpu.make_async_copy(qbuf.at[k], qbuf.at[k], q_recv.at[k]).wait()

        q = qbuf[k, pl.ds(0, q_rows), :]
        top = jnp.full((8, q_rows), -jnp.inf, jnp.float32)
        for c in range(CHUNKS):
            x = lax.dot_general(
                pg[pl.ds(c * chunk, chunk), :], q, (((1,), (1,)), ((), ())), preferred_element_type=jnp.float32
            ).reshape(chunk // 8, 8, q_rows)
            if (c + 1) * chunk > 2 * MIN_COUNT:
                start = c * chunk + 8 * lax.broadcasted_iota(jnp.int32, x.shape, 0)
                x = jnp.where(limit[None] > start, x, -jnp.inf)
            xs[k, c] = x
            top = jnp.maximum(top, jnp.max(x, axis=0))
        top = all_rows(top, jnp.maximum)
        tops[k] = top
        total = jnp.zeros((8, q_rows), jnp.float32)
        for c in range(CHUNKS):
            e = jnp.exp2((xs[k, c] - top[None]) * EXP2_SCALE)
            xs[k, c] = e
            total = total + jnp.sum(e, axis=0)
        totals[k] = total

        return 0

    lax.fori_loop(0, 5, forward, 0)

    parts = []
    total = [all_rows(totals[k], jnp.add) for k in range(5)]
    for k in range(5):
        soft = tops[k] + TAU * jnp.log(total[k])
        hi = soft.astype(jnp.bfloat16).astype(jnp.float32)
        rest = soft - hi
        mid = rest.astype(jnp.bfloat16).astype(jnp.float32)
        parts += [hi, mid, rest - mid]
    parts = jnp.concatenate(parts + [jnp.zeros_like(parts[0])], axis=0).astype(jnp.bfloat16)
    sums = jnp.dot(parts, ones[...], preferred_element_type=jnp.float32).reshape(16, 8, q_rows)
    loss = jnp.zeros((8, q_rows), jnp.float32)
    for k in range(5):
        score = sums[3 * k] + sums[3 * k + 1] + sums[3 * k + 2]
        logit = scale[0] * score + bias[0]
        tag = qbuf[k, pl.ds(q_rows, 16), :].astype(jnp.float32)
        block = jnp.concatenate([tag[0:1], tag[1:2]], axis=1)
        page = jnp.concatenate([tag[2:3], tag[3:4]], axis=1)
        positive = (block == me.astype(jnp.float32)) & (page == parity.astype(jnp.float32))
        sign = jnp.where(positive, 1.0, -1.0)
        t = -sign * logit
        decay = jnp.exp(-jnp.abs(t))
        loss = loss + (jnp.maximum(t, 0.0) + jnp.log1p(decay))
        slope = -sign * scale[0] * jnp.where(t >= 0, 1.0, decay) / (1.0 + decay)
        factors[k] = slope / total[k]

    def l_copy(stage, slot):
        return pltpu.make_async_remote_copy(
            lsend.at[stage], lbufs[stage].at[slot], l_send.at[stage], l_recv.at[stage],
            device_id=(peer(groups[stage][slot]),), device_id_type=MESH,
        )

    def l_wait(stage, sem):
        buf = lbufs[stage].at[pl.ds(1, len(groups[stage]) - 1)]
        pltpu.make_async_copy(buf, buf, sem.at[stage]).wait()

    def l_start(stage, v):
        lsend[stage] = v
        lbufs[stage][0] = v
        for slot in order[stage]:
            l_copy(stage, slot).start()

    def tree(v):
        while v.shape[0] > 1:
            half = v.shape[0] // 2
            v = v[:half] + v[half:]
        return v[0]

    loss = jnp.sum(loss, axis=0, keepdims=True)
    l_start(0, loss[:, :EMB] + loss[:, EMB:])

    def backward(step, _):
        k = 4 - step
        q = qbuf[k, pl.ds(0, q_rows), :]
        factor = factors[k]
        grad_q = jnp.zeros((EMB, q_rows), jnp.float32)
        for c in range(CHUNKS):
            coef = (xs[k, c] * factor[None]).reshape(chunk, q_rows).astype(jnp.bfloat16)
            grad_q = grad_q + jnp.dot(pgt[c], coef, preferred_element_type=jnp.float32)
            part = jnp.dot(coef, q, preferred_element_type=jnp.float32)
            here = pl.ds(c * chunk, chunk)

            gp_out[here, :] += part

        @pl.when(k == 0)
        def _():
            gown[...] = grad_q

        @pl.when(k > 0)
        def _():
            gsend[k] = grad_q.astype(jnp.bfloat16)
            target = me
            for slot in range(1, 5):
                target = target + jnp.where(k == slot, flip[bits[slot - 1]], 0)
            pltpu.make_async_remote_copy(
                gsend.at[k], grecv.at[k], g_send.at[k], g_recv.at[k], device_id=(target,), device_id_type=MESH,
            ).start()

        return 0

    lax.fori_loop(0, 5, backward, 0)

    l_wait(0, l_recv)
    l_start(1, tree(l1[...]))
    grad = gown[...]
    for slot in (1, 2, 3, 4):
        pltpu.make_async_copy(grecv.at[slot], grecv.at[slot], g_recv.at[slot]).wait()
        grad = grad + grecv[slot].astype(jnp.float32)
    gq_out[...] = grad.T
    for slot in range(1, 5):
        q_copy(slot).wait_send()
        pltpu.make_async_copy(gsend.at[slot], gsend.at[slot], g_send.at[slot]).wait()
    l_wait(0, l_send)
    l_wait(1, l_recv)
    loss_out[...] = tree(l2[...])
    l_wait(1, l_send)


def finish(loss, gq, gp, loss_out, gq_out, gp_out, total, sem):
    n_page, emb = gp_out.shape[1:]
    flat = gp_out.reshape(gp_out.shape[0] * n_page, emb)
    copies = [
        pltpu.make_async_copy(gp.at[pl.ds(0, flat.shape[0])], flat, sem.at[0]),
        pltpu.make_async_copy(gq, gq_out, sem.at[1]),
        pltpu.make_async_copy(total, loss_out, sem.at[2]),
    ]
    copies[0].start()
    copies[1].start()
    total[0, 0] = jnp.sum(loss[...]) * (1.0 / (4 * QT))
    copies[2].start()
    for copy in copies:
        copy.wait()


def per_device(n_dev, queries, pages, counts, labels, logit_scale, logit_bias):
    n_query, q_tok, emb = queries.shape
    n_page, page_len, _ = pages.shape
    q_rows = n_query * q_tok
    p_rows = n_page * page_len
    p_pad = (p_rows + 16 * CHUNKS - 1) // (16 * CHUNKS) * (16 * CHUNKS)
    sizes = [len(g) for g in loss_groups(n_dev.bit_length() - 1)]
    vmem = pl.BlockSpec(memory_space=pltpu.VMEM)
    hbm = pl.BlockSpec(memory_space=pltpu.HBM)
    bf16, f32 = jnp.bfloat16, jnp.float32
    dma = pltpu.SemaphoreType.DMA
    gp_shape = jax.ShapeDtypeStruct((page_len, n_page, emb), f32)
    gq_shape = jax.ShapeDtypeStruct((q_rows, emb), f32)
    operands = (
        queries.reshape(q_rows, emb),
        jnp.transpose(pages, (1, 0, 2)),
        counts,
        labels,
        logit_scale.reshape(1),
        logit_bias.reshape(1),
    )
    parts = pl.pallas_call(
        lambda *refs: kernel(n_dev, q_rows, p_rows, *refs),
        out_shape=(jax.ShapeDtypeStruct((1, emb), f32), gq_shape, jax.ShapeDtypeStruct((p_pad, emb), f32)),
        in_specs=[hbm] * 6,
        out_specs=(vmem, vmem, vmem),
        scratch_shapes=[
            pltpu.SMEM(counts.shape, jnp.int32),
            pltpu.SMEM(labels.shape, jnp.int32),
            pltpu.SMEM((1,), f32),
            pltpu.SMEM((1,), f32),
            pltpu.VMEM((5, q_rows + 16, emb), bf16),
            pltpu.VMEM((p_pad, emb), bf16),
            pltpu.VMEM((CHUNKS, emb, p_pad // CHUNKS), bf16),
            pltpu.VMEM((5, CHUNKS, p_pad // (8 * CHUNKS), 8, q_rows), f32),
            pltpu.VMEM((5, 8, q_rows), f32),
            pltpu.VMEM((5, 8, q_rows), f32),
            pltpu.VMEM((5, 8, q_rows), f32),
            pltpu.VMEM((emb, q_rows), f32),
            pltpu.VMEM((5, emb, q_rows), bf16),
            pltpu.VMEM((5, emb, q_rows), bf16),
            pltpu.VMEM((q_rows, q_rows), bf16),
            pltpu.VMEM((2, 1, emb), f32),
            *[pltpu.VMEM((n, 1, emb), f32) for n in sizes],
            dma((6,)),
            dma((5,)),
            dma((5,)),
            dma((5,)),
            dma((5,)),
            dma((2,)),
            dma((2,)),
        ],
        compiler_params=pltpu.CompilerParams(
            collective_id=0, has_side_effects=True, vmem_limit_bytes=40 * 1024 * 1024
        ),
    )(*[pltpu.with_memory_space_constraint(x, pltpu.HBM) for x in operands[:4]], *operands[4:])
    loss, grad_q, grad_p = pl.pallas_call(
        finish,
        out_shape=(jax.ShapeDtypeStruct((1, 1), f32), gq_shape, gp_shape),
        in_specs=[vmem] * 3,
        out_specs=(hbm, hbm, hbm),
        scratch_shapes=[pltpu.SMEM((1, 1), f32), dma((3,))],
        compiler_params=pltpu.CompilerParams(vmem_limit_bytes=16 * 1024 * 1024),
    )(*parts)
    return loss.reshape(()), grad_q.reshape(n_query, q_tok, emb), jnp.transpose(grad_p, (1, 0, 2))


def solution(mesh):
    n_dev = mesh.shape["dp"]
    placed = (P("dp", None, None), P("dp", None, None), P("dp"), P("dp"), P(), P())
    return jax.shard_map(
        lambda *args: per_device(n_dev, *args),
        mesh=mesh,
        in_specs=placed,
        out_specs=(P(), P("dp", None, None), P("dp", None, None)),
        check_vma=False,
    )
```

```python
import jax
import jax.numpy as jnp
from jax import lax
from jax.experimental import pallas as pl
from jax.experimental.pallas import tpu as pltpu
from jax.sharding import PartitionSpec as P

EMB = 128
QT = 32
TAU = 0.1
EXP2_SCALE = 1.4426950408889634 / TAU
MIN_COUNT = 700
CHUNKS = 3
MESH = pl.DeviceIdType.MESH


def combos(bits):
    return [sum(1 << b for i, b in enumerate(bits) if s >> i & 1) for s in range(1 << len(bits))]


def far_first(offsets, far):
    return sorted(range(1, len(offsets)), key=lambda s: (-sum(far[b] for b in range(8) if offsets[s] >> b & 1), s))


def axes(n_bits):
    return [[0], [1, 2], [3, 4, 5], [6, 7]] if n_bits == 8 else [[0], [1], [2], [3]]


def loss_groups(n_bits):
    core, x, z, y = axes(n_bits)
    return [combos(core + x + y), combos(z)]


def kernel(
    n_dev, q_rows, p_rows,
    q_hbm, p_hbm, counts_hbm, labels_hbm, scale_hbm, bias_hbm,
    loss_out, gq_out, gp_out,
    counts, labels, scale, bias,
    qbuf, pg, pgt, xs, tops, totals, factors, gown, gsend, grecv, ones, lsend, l1, l2,
    local_sem, q_send, q_recv, g_send, g_recv, l_send, l_recv, column_sem, core_sem,
):
    me = lax.axis_index("dp")
    n_bits = n_dev.bit_length() - 1
    flip = [(1 << b) - 2 * (1 << b) * ((me // (1 << b)) % 2) for b in range(n_bits)]

    def peer(offset):
        out = me
        for b in range(n_bits):
            if offset >> b & 1:
                out = out + flip[b]
        return out

    bits = [n_bits - 2, n_bits - 1, n_bits - 3, n_bits - 4]
    groups = loss_groups(n_bits)
    far = [0.5, 1, 2, 1, 2, 4, 1, 2]
    lbufs = (l1, l2)
    order = [far_first(g, far) for g in groups]
    p_pad = pg.shape[0]
    chunk = p_pad // CHUNKS

    barrier = pltpu.get_barrier_semaphore()

    def greet(offset):
        pl.semaphore_signal(barrier, inc=1, device_id=(peer(offset),), device_id_type=MESH)

    core, _, _, column = [combos(axis)[1:] for axis in axes(n_bits)]
    first = [1 << bits[slot - 1] for slot in (3, 4, 2, 1)]
    others = [d for axis in axes(n_bits) for d in combos(axis)[1:] if d not in first]
    for d in first:
        greet(d)

    pg[pl.ds(p_pad - 16, 16), :] = jnp.zeros((16, EMB), jnp.bfloat16)
    local = [
        pltpu.make_async_copy(src, dst, local_sem.at[i])
        for i, (src, dst) in enumerate(
            [
                (labels_hbm, labels),
                (q_hbm, qbuf.at[0, pl.ds(0, q_rows)]),
                (p_hbm.reshape(p_rows, EMB), pg.at[pl.ds(0, p_rows)]),
                (counts_hbm, counts),
                (scale_hbm, scale),
                (bias_hbm, bias),
            ]
        )
    ]
    for d in others:
        greet(d)
    for copy in local:
        copy.start()

    local[0].wait()
    row = lax.broadcasted_iota(jnp.int32, (16, EMB), 0)
    lane = lax.broadcasted_iota(jnp.int32, (16, EMB), 1)
    which = (row & 1) * (EMB // QT) + lane // QT
    label = jnp.zeros((16, EMB), jnp.int32)
    for q in range(q_rows // QT):
        label = jnp.where(which == q, labels[q], label)
    qbuf[0, pl.ds(q_rows, 16), :] = jnp.where(row < 2, label >> 1, label & 1).astype(jnp.float32).astype(jnp.bfloat16)

    local[1].wait()
    pl.semaphore_wait(barrier, len(first) + len(others))

    def q_copy(slot):
        return pltpu.make_async_remote_copy(
            qbuf.at[0], qbuf.at[slot], q_send.at[slot], q_recv.at[slot],
            device_id=(peer(1 << bits[slot - 1]),), device_id_type=MESH,
        )

    for slot in (3, 4, 2, 1):
        q_copy(slot).start()

    def vouch(sem, offsets):
        for d in offsets:
            pl.semaphore_signal(sem, inc=1, device_id=(peer(d),), device_id_type=MESH)

    vouch(column_sem, column)

    group_row = lax.broadcasted_iota(jnp.int32, (q_rows, q_rows), 0) // QT
    group_col = lax.broadcasted_iota(jnp.int32, (q_rows, q_rows), 1) // QT
    ones[...] = jnp.where(group_row == group_col, 1.0, 0.0).astype(jnp.bfloat16)
    sub = lax.broadcasted_iota(jnp.int32, (8, q_rows), 0)
    parity = sub & 1
    for copy in local[2:]:
        copy.wait()
    limit = 2 * jnp.where(parity == 0, counts[0], counts[1]) - sub

    for c in range(CHUNKS):
        pgt[c] = pg[pl.ds(c * chunk, chunk), :].astype(jnp.float32).T.astype(jnp.bfloat16)

    gp_out[...] = jnp.zeros_like(gp_out)

    def all_rows(vec, op):
        vec = op(vec, pltpu.roll(vec, 2, 0))
        return op(vec, pltpu.roll(vec, 4, 0))

    def forward(k, _):
        @pl.when(k > 0)
        def _():
            pltpu.make_async_copy(qbuf.at[k], qbuf.at[k], q_recv.at[k]).wait()

        @pl.when(k == 2)
        def _():
            pl.semaphore_wait(column_sem, len(column))
            vouch(core_sem, core)

        q = qbuf[k, pl.ds(0, q_rows), :]
        top = jnp.full((8, q_rows), -jnp.inf, jnp.float32)
        for c in range(CHUNKS):
            x = lax.dot_general(
                pg[pl.ds(c * chunk, chunk), :], q, (((1,), (1,)), ((), ())), preferred_element_type=jnp.float32
            ).reshape(chunk // 8, 8, q_rows)
            if (c + 1) * chunk > 2 * MIN_COUNT:
                start = c * chunk + 8 * lax.broadcasted_iota(jnp.int32, x.shape, 0)
                x = jnp.where(limit[None] > start, x, -jnp.inf)
            xs[k, c] = x
            top = jnp.maximum(top, jnp.max(x, axis=0))
        top = all_rows(top, jnp.maximum)
        tops[k] = top
        total = jnp.zeros((8, q_rows), jnp.float32)
        for c in range(CHUNKS):
            e = jnp.exp2((xs[k, c] - top[None]) * EXP2_SCALE)
            xs[k, c] = e
            total = total + jnp.sum(e, axis=0)
        totals[k] = total

        return 0

    lax.fori_loop(0, 5, forward, 0)

    parts = []
    total = [all_rows(totals[k], jnp.add) for k in range(5)]
    for k in range(5):
        soft = tops[k] + TAU * jnp.log(total[k])
        hi = soft.astype(jnp.bfloat16).astype(jnp.float32)
        rest = soft - hi
        mid = rest.astype(jnp.bfloat16).astype(jnp.float32)
        parts += [hi, mid, rest - mid]
    parts = jnp.concatenate(parts + [jnp.zeros_like(parts[0])], axis=0).astype(jnp.bfloat16)
    sums = jnp.dot(parts, ones[...], preferred_element_type=jnp.float32).reshape(16, 8, q_rows)
    loss = jnp.zeros((8, q_rows), jnp.float32)
    for k in range(5):
        score = sums[3 * k] + sums[3 * k + 1] + sums[3 * k + 2]
        logit = scale[0] * score + bias[0]
        tag = qbuf[k, pl.ds(q_rows, 16), :].astype(jnp.float32)
        block = jnp.concatenate([tag[0:1], tag[1:2]], axis=1)
        page = jnp.concatenate([tag[2:3], tag[3:4]], axis=1)
        positive = (block == me.astype(jnp.float32)) & (page == parity.astype(jnp.float32))
        sign = jnp.where(positive, 1.0, -1.0)
        t = -sign * logit
        decay = jnp.exp(-jnp.abs(t))
        loss = loss + (jnp.maximum(t, 0.0) + jnp.log1p(decay))
        slope = -sign * scale[0] * jnp.where(t >= 0, 1.0, decay) / (1.0 + decay)
        factors[k] = slope / total[k]

    def l_copy(stage, slot):
        return pltpu.make_async_remote_copy(
            lsend.at[stage], lbufs[stage].at[slot], l_send.at[stage], l_recv.at[stage],
            device_id=(peer(groups[stage][slot]),), device_id_type=MESH,
        )

    def l_wait(stage, sem):
        buf = lbufs[stage].at[pl.ds(1, len(groups[stage]) - 1)]
        pltpu.make_async_copy(buf, buf, sem.at[stage]).wait()

    def l_start(stage, v):
        lsend[stage] = v
        lbufs[stage][0] = v
        for slot in order[stage]:
            l_copy(stage, slot).start()

    def tree(v):
        while v.shape[0] > 1:
            half = v.shape[0] // 2
            v = v[:half] + v[half:]
        return v[0]

    loss = jnp.sum(loss, axis=0, keepdims=True)
    pl.semaphore_wait(core_sem, len(core))
    l_start(0, loss[:, :EMB] + loss[:, EMB:])

    def backward(step, _):
        k = 4 - step
        q = qbuf[k, pl.ds(0, q_rows), :]
        factor = factors[k]
        grad_q = jnp.zeros((EMB, q_rows), jnp.float32)
        for c in range(CHUNKS):
            coef = (xs[k, c] * factor[None]).reshape(chunk, q_rows).astype(jnp.bfloat16)
            grad_q = grad_q + jnp.dot(pgt[c], coef, preferred_element_type=jnp.float32)
            part = jnp.dot(coef, q, preferred_element_type=jnp.float32)
            here = pl.ds(c * chunk, chunk)

            gp_out[here, :] += part

        @pl.when(k == 0)
        def _():
            gown[...] = grad_q

        @pl.when(k > 0)
        def _():
            gsend[k] = grad_q.astype(jnp.bfloat16)
            target = me
            for slot in range(1, 5):
                target = target + jnp.where(k == slot, flip[bits[slot - 1]], 0)
            pltpu.make_async_remote_copy(
                gsend.at[k], grecv.at[k], g_send.at[k], g_recv.at[k], device_id=(target,), device_id_type=MESH,
            ).start()

        return 0

    lax.fori_loop(0, 5, backward, 0)

    l_wait(0, l_recv)
    l_start(1, tree(l1[...]))
    grad = gown[...]
    for slot in (1, 2, 3, 4):
        pltpu.make_async_copy(grecv.at[slot], grecv.at[slot], g_recv.at[slot]).wait()
        grad = grad + grecv[slot].astype(jnp.float32)
    gq_out[...] = grad.T
    for slot in range(1, 5):
        q_copy(slot).wait_send()
        pltpu.make_async_copy(gsend.at[slot], gsend.at[slot], g_send.at[slot]).wait()
    l_wait(0, l_send)
    l_wait(1, l_recv)
    loss_out[...] = tree(l2[...])
    l_wait(1, l_send)


def finish(loss, gq, gp, loss_out, gq_out, gp_out, total, sem):
    n_page, emb = gp_out.shape[1:]
    flat = gp_out.reshape(gp_out.shape[0] * n_page, emb)
    copies = [
        pltpu.make_async_copy(gp.at[pl.ds(0, flat.shape[0])], flat, sem.at[0]),
        pltpu.make_async_copy(gq, gq_out, sem.at[1]),
        pltpu.make_async_copy(total, loss_out, sem.at[2]),
    ]
    copies[0].start()
    copies[1].start()
    total[0, 0] = jnp.sum(loss[...]) * (1.0 / (4 * QT))
    copies[2].start()
    for copy in copies:
        copy.wait()


def per_device(n_dev, queries, pages, counts, labels, logit_scale, logit_bias):
    n_query, q_tok, emb = queries.shape
    n_page, page_len, _ = pages.shape
    q_rows = n_query * q_tok
    p_rows = n_page * page_len
    p_pad = (p_rows + 16 * CHUNKS - 1) // (16 * CHUNKS) * (16 * CHUNKS)
    sizes = [len(g) for g in loss_groups(n_dev.bit_length() - 1)]
    vmem = pl.BlockSpec(memory_space=pltpu.VMEM)
    hbm = pl.BlockSpec(memory_space=pltpu.HBM)
    bf16, f32 = jnp.bfloat16, jnp.float32
    dma = pltpu.SemaphoreType.DMA
    gp_shape = jax.ShapeDtypeStruct((page_len, n_page, emb), f32)
    gq_shape = jax.ShapeDtypeStruct((q_rows, emb), f32)
    operands = (
        queries.reshape(q_rows, emb),
        jnp.transpose(pages, (1, 0, 2)),
        counts,
        labels,
        logit_scale.reshape(1),
        logit_bias.reshape(1),
    )
    parts = pl.pallas_call(
        lambda *refs: kernel(n_dev, q_rows, p_rows, *refs),
        out_shape=(jax.ShapeDtypeStruct((1, emb), f32), gq_shape, jax.ShapeDtypeStruct((p_pad, emb), f32)),
        in_specs=[hbm] * 6,
        out_specs=(vmem, vmem, vmem),
        scratch_shapes=[
            pltpu.SMEM(counts.shape, jnp.int32),
            pltpu.SMEM(labels.shape, jnp.int32),
            pltpu.SMEM((1,), f32),
            pltpu.SMEM((1,), f32),
            pltpu.VMEM((5, q_rows + 16, emb), bf16),
            pltpu.VMEM((p_pad, emb), bf16),
            pltpu.VMEM((CHUNKS, emb, p_pad // CHUNKS), bf16),
            pltpu.VMEM((5, CHUNKS, p_pad // (8 * CHUNKS), 8, q_rows), f32),
            pltpu.VMEM((5, 8, q_rows), f32),
            pltpu.VMEM((5, 8, q_rows), f32),
            pltpu.VMEM((5, 8, q_rows), f32),
            pltpu.VMEM((emb, q_rows), f32),
            pltpu.VMEM((5, emb, q_rows), bf16),
            pltpu.VMEM((5, emb, q_rows), bf16),
            pltpu.VMEM((q_rows, q_rows), bf16),
            pltpu.VMEM((2, 1, emb), f32),
            *[pltpu.VMEM((n, 1, emb), f32) for n in sizes],
            dma((6,)),
            dma((5,)),
            dma((5,)),
            dma((5,)),
            dma((5,)),
            dma((2,)),
            dma((2,)),
            pltpu.SemaphoreType.REGULAR,
            pltpu.SemaphoreType.REGULAR,
        ],
        compiler_params=pltpu.CompilerParams(
            collective_id=0, has_side_effects=True, vmem_limit_bytes=40 * 1024 * 1024
        ),
    )(*[pltpu.with_memory_space_constraint(x, pltpu.HBM) for x in operands[:4]], *operands[4:])
    loss, grad_q, grad_p = pl.pallas_call(
        finish,
        out_shape=(jax.ShapeDtypeStruct((1, 1), f32), gq_shape, gp_shape),
        in_specs=[vmem] * 3,
        out_specs=(hbm, hbm, hbm),
        scratch_shapes=[pltpu.SMEM((1, 1), f32), dma((3,))],
        compiler_params=pltpu.CompilerParams(vmem_limit_bytes=16 * 1024 * 1024),
    )(*parts)
    return loss.reshape(()), grad_q.reshape(n_query, q_tok, emb), jnp.transpose(grad_p, (1, 0, 2))


def solution(mesh):
    n_dev = mesh.shape["dp"]
    placed = (P("dp", None, None), P("dp", None, None), P("dp"), P("dp"), P(), P())
    return jax.shard_map(
        lambda *args: per_device(n_dev, *args),
        mesh=mesh,
        in_specs=placed,
        out_specs=(P(), P("dp", None, None), P("dp", None, None)),
        check_vma=False,
    )
```

```python
import jax
import jax.numpy as jnp
from jax import lax
from jax.experimental import pallas as pl
from jax.experimental.pallas import tpu as pltpu
from jax.sharding import PartitionSpec as P

EMB = 128
QT = 32
TAU = 0.1
EXP2_SCALE = 1.4426950408889634 / TAU
MIN_COUNT = 700
CHUNKS = 3
MESH = pl.DeviceIdType.MESH


def combos(bits):
    return [sum(1 << b for i, b in enumerate(bits) if s >> i & 1) for s in range(1 << len(bits))]


def far_first(offsets, far):
    return sorted(range(1, len(offsets)), key=lambda s: (-sum(far[b] for b in range(8) if offsets[s] >> b & 1), s))


def axes(n_bits):
    return [[0], [1, 2], [3, 4, 5], [6, 7]] if n_bits == 8 else [[0], [1], [2], [3]]


def loss_groups(n_bits):
    core, x, z, y = axes(n_bits)
    return [combos(core + x + y), combos(z)]


def kernel(
    n_dev, q_rows, p_rows,
    q_hbm, p_hbm, counts_hbm, labels_hbm, scale_hbm, bias_hbm,
    loss_out, gq_out, gp_out,
    counts, labels, scale, bias,
    qbuf, pg, pgt, xs, tops, totals, factors, gown, gsend, grecv, ones, lsend, l1, l2,
    local_sem, q_send, q_recv, g_send, g_recv, l_send, l_recv, column_sem, core_sem,
):
    me = lax.axis_index("dp")
    n_bits = n_dev.bit_length() - 1
    flip = [(1 << b) - 2 * (1 << b) * ((me // (1 << b)) % 2) for b in range(n_bits)]

    def peer(offset):
        out = me
        for b in range(n_bits):
            if offset >> b & 1:
                out = out + flip[b]
        return out

    bits = [n_bits - 2, n_bits - 1, n_bits - 3, n_bits - 4]
    groups = loss_groups(n_bits)
    far = [0.5, 1, 2, 1, 2, 4, 1, 2]
    lbufs = (l1, l2)
    order = [far_first(g, far) for g in groups]
    p_pad = pg.shape[0]
    chunk = p_pad // CHUNKS

    barrier = pltpu.get_barrier_semaphore()

    def greet(offset):
        pl.semaphore_signal(barrier, inc=1, device_id=(peer(offset),), device_id_type=MESH)

    core, _, _, column = [combos(axis)[1:] for axis in axes(n_bits)]
    first = [1 << bits[slot - 1] for slot in (3, 4, 2, 1)]
    others = [d for axis in axes(n_bits) for d in combos(axis)[1:] if d not in first]
    for d in first:
        greet(d)

    pg[pl.ds(p_pad - 16, 16), :] = jnp.zeros((16, EMB), jnp.bfloat16)
    local = [
        pltpu.make_async_copy(src, dst, local_sem.at[i])
        for i, (src, dst) in enumerate(
            [
                (labels_hbm, labels),
                (q_hbm, qbuf.at[0, pl.ds(0, q_rows)]),
                (p_hbm.reshape(p_rows, EMB), pg.at[pl.ds(0, p_rows)]),
                (counts_hbm, counts),
                (scale_hbm, scale),
                (bias_hbm, bias),
            ]
        )
    ]
    for d in others:
        greet(d)
    for copy in local:
        copy.start()

    local[0].wait()
    row = lax.broadcasted_iota(jnp.int32, (16, EMB), 0)
    lane = lax.broadcasted_iota(jnp.int32, (16, EMB), 1)
    which = (row & 1) * (EMB // QT) + lane // QT
    label = jnp.zeros((16, EMB), jnp.int32)
    for q in range(q_rows // QT):
        label = jnp.where(which == q, labels[q], label)
    qbuf[0, pl.ds(q_rows, 16), :] = jnp.where(row < 2, label >> 1, label & 1).astype(jnp.float32).astype(jnp.bfloat16)

    local[1].wait()
    pl.semaphore_wait(barrier, len(first) + len(others))

    def q_copy(slot):
        return pltpu.make_async_remote_copy(
            qbuf.at[0], qbuf.at[slot], q_send.at[slot], q_recv.at[slot],
            device_id=(peer(1 << bits[slot - 1]),), device_id_type=MESH,
        )

    for slot in (3, 4, 2, 1):
        q_copy(slot).start()

    def vouch(sem, offsets):
        for d in offsets:
            pl.semaphore_signal(sem, inc=1, device_id=(peer(d),), device_id_type=MESH)

    vouch(column_sem, column)

    group_row = lax.broadcasted_iota(jnp.int32, (q_rows, q_rows), 0) // QT
    group_col = lax.broadcasted_iota(jnp.int32, (q_rows, q_rows), 1) // QT
    ones[...] = jnp.where(group_row == group_col, 1.0, 0.0).astype(jnp.bfloat16)
    sub = lax.broadcasted_iota(jnp.int32, (8, q_rows), 0)
    parity = sub & 1
    for copy in local[2:]:
        copy.wait()
    limit = 2 * jnp.where(parity == 0, counts[0], counts[1]) - sub

    for c in range(CHUNKS):
        pgt[c] = pg[pl.ds(c * chunk, chunk), :].astype(jnp.float32).T.astype(jnp.bfloat16)

    gp_out[...] = jnp.zeros_like(gp_out)

    def all_rows(vec, op):
        vec = op(vec, pltpu.roll(vec, 2, 0))
        return op(vec, pltpu.roll(vec, 4, 0))

    def forward(k):
        q = qbuf[k, pl.ds(0, q_rows), :]
        top = jnp.full((8, q_rows), -jnp.inf, jnp.float32)
        for c in range(CHUNKS):
            x = lax.dot_general(
                pg[pl.ds(c * chunk, chunk), :], q, (((1,), (1,)), ((), ())), preferred_element_type=jnp.float32
            ).reshape(chunk // 8, 8, q_rows)
            if (c + 1) * chunk > 2 * MIN_COUNT:
                start = c * chunk + 8 * lax.broadcasted_iota(jnp.int32, x.shape, 0)
                x = jnp.where(limit[None] > start, x, -jnp.inf)
            xs[k, c] = x
            top = jnp.maximum(top, jnp.max(x, axis=0))
        top = all_rows(top, jnp.maximum)
        tops[k] = top
        total = jnp.zeros((8, q_rows), jnp.float32)
        for c in range(CHUNKS):
            e = jnp.exp2((xs[k, c] - top[None]) * EXP2_SCALE)
            xs[k, c] = e
            total = total + jnp.sum(e, axis=0)
        totals[k] = total

    def pair(turn, _):
        for k in (2 * turn + 1, 2 * turn + 2):
            pltpu.make_async_copy(qbuf.at[k], qbuf.at[k], q_recv.at[k]).wait()

        @pl.when(turn == 0)
        def _():
            pl.semaphore_wait(column_sem, len(column))
            vouch(core_sem, core)

        forward(2 * turn + 1)
        forward(2 * turn + 2)
        return 0

    forward(0)
    lax.fori_loop(0, 2, pair, 0)

    parts = []
    total = [all_rows(totals[k], jnp.add) for k in range(5)]
    for k in range(5):
        soft = tops[k] + TAU * jnp.log(total[k])
        hi = soft.astype(jnp.bfloat16).astype(jnp.float32)
        rest = soft - hi
        mid = rest.astype(jnp.bfloat16).astype(jnp.float32)
        parts += [hi, mid, rest - mid]
    parts = jnp.concatenate(parts + [jnp.zeros_like(parts[0])], axis=0).astype(jnp.bfloat16)
    sums = jnp.dot(parts, ones[...], preferred_element_type=jnp.float32).reshape(16, 8, q_rows)
    loss = jnp.zeros((8, q_rows), jnp.float32)
    for k in range(5):
        score = sums[3 * k] + sums[3 * k + 1] + sums[3 * k + 2]
        logit = scale[0] * score + bias[0]
        tag = qbuf[k, pl.ds(q_rows, 16), :].astype(jnp.float32)
        block = jnp.concatenate([tag[0:1], tag[1:2]], axis=1)
        page = jnp.concatenate([tag[2:3], tag[3:4]], axis=1)
        positive = (block == me.astype(jnp.float32)) & (page == parity.astype(jnp.float32))
        sign = jnp.where(positive, 1.0, -1.0)
        t = -sign * logit
        decay = jnp.exp(-jnp.abs(t))
        loss = loss + (jnp.maximum(t, 0.0) + jnp.log1p(decay))
        slope = -sign * scale[0] * jnp.where(t >= 0, 1.0, decay) / (1.0 + decay)
        factors[k] = slope / total[k]

    def l_copy(stage, slot):
        return pltpu.make_async_remote_copy(
            lsend.at[stage], lbufs[stage].at[slot], l_send.at[stage], l_recv.at[stage],
            device_id=(peer(groups[stage][slot]),), device_id_type=MESH,
        )

    def l_wait(stage, sem):
        buf = lbufs[stage].at[pl.ds(1, len(groups[stage]) - 1)]
        pltpu.make_async_copy(buf, buf, sem.at[stage]).wait()

    def l_start(stage, v):
        lsend[stage] = v
        lbufs[stage][0] = v
        for slot in order[stage]:
            l_copy(stage, slot).start()

    def tree(v):
        while v.shape[0] > 1:
            half = v.shape[0] // 2
            v = v[:half] + v[half:]
        return v[0]

    loss = jnp.sum(loss, axis=0, keepdims=True)
    pl.semaphore_wait(core_sem, len(core))
    l_start(0, loss[:, :EMB] + loss[:, EMB:])

    def backward(step, _):
        k = 4 - step
        q = qbuf[k, pl.ds(0, q_rows), :]
        factor = factors[k]
        grad_q = jnp.zeros((EMB, q_rows), jnp.float32)
        for c in range(CHUNKS):
            coef = (xs[k, c] * factor[None]).reshape(chunk, q_rows).astype(jnp.bfloat16)
            grad_q = grad_q + jnp.dot(pgt[c], coef, preferred_element_type=jnp.float32)
            part = jnp.dot(coef, q, preferred_element_type=jnp.float32)
            here = pl.ds(c * chunk, chunk)

            gp_out[here, :] += part

        @pl.when(k == 0)
        def _():
            gown[...] = grad_q

        @pl.when(k > 0)
        def _():
            gsend[k] = grad_q.astype(jnp.bfloat16)
            target = me
            for slot in range(1, 5):
                target = target + jnp.where(k == slot, flip[bits[slot - 1]], 0)
            pltpu.make_async_remote_copy(
                gsend.at[k], grecv.at[k], g_send.at[k], g_recv.at[k], device_id=(target,), device_id_type=MESH,
            ).start()

        return 0

    lax.fori_loop(0, 5, backward, 0)

    l_wait(0, l_recv)
    l_start(1, tree(l1[...]))
    grad = gown[...]
    for slot in (1, 2, 3, 4):
        pltpu.make_async_copy(grecv.at[slot], grecv.at[slot], g_recv.at[slot]).wait()
        grad = grad + grecv[slot].astype(jnp.float32)
    gq_out[...] = grad.T
    for slot in range(1, 5):
        q_copy(slot).wait_send()
        pltpu.make_async_copy(gsend.at[slot], gsend.at[slot], g_send.at[slot]).wait()
    l_wait(0, l_send)
    l_wait(1, l_recv)
    loss_out[...] = tree(l2[...])
    l_wait(1, l_send)


def finish(loss, gq, gp, loss_out, gq_out, gp_out, total, sem):
    n_page, emb = gp_out.shape[1:]
    flat = gp_out.reshape(gp_out.shape[0] * n_page, emb)
    copies = [
        pltpu.make_async_copy(gp.at[pl.ds(0, flat.shape[0])], flat, sem.at[0]),
        pltpu.make_async_copy(gq, gq_out, sem.at[1]),
        pltpu.make_async_copy(total, loss_out, sem.at[2]),
    ]
    copies[0].start()
    copies[1].start()
    total[0, 0] = jnp.sum(loss[...]) * (1.0 / (4 * QT))
    copies[2].start()
    for copy in copies:
        copy.wait()


def per_device(n_dev, queries, pages, counts, labels, logit_scale, logit_bias):
    n_query, q_tok, emb = queries.shape
    n_page, page_len, _ = pages.shape
    q_rows = n_query * q_tok
    p_rows = n_page * page_len
    p_pad = (p_rows + 16 * CHUNKS - 1) // (16 * CHUNKS) * (16 * CHUNKS)
    sizes = [len(g) for g in loss_groups(n_dev.bit_length() - 1)]
    vmem = pl.BlockSpec(memory_space=pltpu.VMEM)
    hbm = pl.BlockSpec(memory_space=pltpu.HBM)
    bf16, f32 = jnp.bfloat16, jnp.float32
    dma = pltpu.SemaphoreType.DMA
    gp_shape = jax.ShapeDtypeStruct((page_len, n_page, emb), f32)
    gq_shape = jax.ShapeDtypeStruct((q_rows, emb), f32)
    operands = (
        queries.reshape(q_rows, emb),
        jnp.transpose(pages, (1, 0, 2)),
        counts,
        labels,
        logit_scale.reshape(1),
        logit_bias.reshape(1),
    )
    parts = pl.pallas_call(
        lambda *refs: kernel(n_dev, q_rows, p_rows, *refs),
        out_shape=(jax.ShapeDtypeStruct((1, emb), f32), gq_shape, jax.ShapeDtypeStruct((p_pad, emb), f32)),
        in_specs=[hbm] * 6,
        out_specs=(vmem, vmem, vmem),
        scratch_shapes=[
            pltpu.SMEM(counts.shape, jnp.int32),
            pltpu.SMEM(labels.shape, jnp.int32),
            pltpu.SMEM((1,), f32),
            pltpu.SMEM((1,), f32),
            pltpu.VMEM((5, q_rows + 16, emb), bf16),
            pltpu.VMEM((p_pad, emb), bf16),
            pltpu.VMEM((CHUNKS, emb, p_pad // CHUNKS), bf16),
            pltpu.VMEM((5, CHUNKS, p_pad // (8 * CHUNKS), 8, q_rows), f32),
            pltpu.VMEM((5, 8, q_rows), f32),
            pltpu.VMEM((5, 8, q_rows), f32),
            pltpu.VMEM((5, 8, q_rows), f32),
            pltpu.VMEM((emb, q_rows), f32),
            pltpu.VMEM((5, emb, q_rows), bf16),
            pltpu.VMEM((5, emb, q_rows), bf16),
            pltpu.VMEM((q_rows, q_rows), bf16),
            pltpu.VMEM((2, 1, emb), f32),
            *[pltpu.VMEM((n, 1, emb), f32) for n in sizes],
            dma((6,)),
            dma((5,)),
            dma((5,)),
            dma((5,)),
            dma((5,)),
            dma((2,)),
            dma((2,)),
            pltpu.SemaphoreType.REGULAR,
            pltpu.SemaphoreType.REGULAR,
        ],
        compiler_params=pltpu.CompilerParams(
            collective_id=0, has_side_effects=True, vmem_limit_bytes=40 * 1024 * 1024
        ),
    )(*[pltpu.with_memory_space_constraint(x, pltpu.HBM) for x in operands[:4]], *operands[4:])
    loss, grad_q, grad_p = pl.pallas_call(
        finish,
        out_shape=(jax.ShapeDtypeStruct((1, 1), f32), gq_shape, gp_shape),
        in_specs=[vmem] * 3,
        out_specs=(hbm, hbm, hbm),
        scratch_shapes=[pltpu.SMEM((1, 1), f32), dma((3,))],
        compiler_params=pltpu.CompilerParams(vmem_limit_bytes=16 * 1024 * 1024),
    )(*parts)
    return loss.reshape(()), grad_q.reshape(n_query, q_tok, emb), jnp.transpose(grad_p, (1, 0, 2))


def solution(mesh):
    n_dev = mesh.shape["dp"]
    placed = (P("dp", None, None), P("dp", None, None), P("dp"), P("dp"), P(), P())
    return jax.shard_map(
        lambda *args: per_device(n_dev, *args),
        mesh=mesh,
        in_specs=placed,
        out_specs=(P(), P("dp", None, None), P("dp", None, None)),
        check_vma=False,
    )
```

```python
import jax
import jax.numpy as jnp
from jax import lax
from jax.experimental import pallas as pl
from jax.experimental.pallas import tpu as pltpu
from jax.sharding import PartitionSpec as P

EMB = 128
QT = 32
TAU = 0.1
EXP2_SCALE = 1.4426950408889634 / TAU
MIN_COUNT = 700
CHUNKS = 3
MESH = pl.DeviceIdType.MESH


def combos(bits):
    return [sum(1 << b for i, b in enumerate(bits) if s >> i & 1) for s in range(1 << len(bits))]


def far_first(offsets, far):
    return sorted(range(1, len(offsets)), key=lambda s: (-sum(far[b] for b in range(8) if offsets[s] >> b & 1), s))


def axes(n_bits):
    return [[0], [1, 2], [3, 4, 5], [6, 7]] if n_bits == 8 else [[0], [1], [2], [3]]


def loss_groups(n_bits):
    core, x, z, y = axes(n_bits)
    return [combos(core + x + y), combos(z)]


def kernel(
    n_dev, q_rows, p_rows,
    q_hbm, p_hbm, counts_hbm, labels_hbm, scale_hbm, bias_hbm,
    loss_out, gq_out, gp_out,
    counts, labels, scale, bias,
    qbuf, pg, pgt, xs, tops, totals, factors, losses, gown, gsend, grecv, ones, lsend, l1, l2,
    local_sem, q_send, q_recv, g_send, g_recv, l_send, l_recv, column_sem, core_sem,
):
    me = lax.axis_index("dp")
    n_bits = n_dev.bit_length() - 1
    flip = [(1 << b) - 2 * (1 << b) * ((me // (1 << b)) % 2) for b in range(n_bits)]

    def peer(offset):
        out = me
        for b in range(n_bits):
            if offset >> b & 1:
                out = out + flip[b]
        return out

    bits = [n_bits - 2, n_bits - 1, n_bits - 3, n_bits - 4]
    groups = loss_groups(n_bits)
    far = [0.5, 1, 2, 1, 2, 4, 1, 2]
    lbufs = (l1, l2)
    order = [far_first(g, far) for g in groups]
    p_pad = pg.shape[0]
    chunk = p_pad // CHUNKS

    barrier = pltpu.get_barrier_semaphore()

    def greet(offset):
        pl.semaphore_signal(barrier, inc=1, device_id=(peer(offset),), device_id_type=MESH)

    core, _, _, column = [combos(axis)[1:] for axis in axes(n_bits)]
    first = [1 << bits[slot - 1] for slot in (3, 4, 2, 1)]
    others = [d for axis in axes(n_bits) for d in combos(axis)[1:] if d not in first]
    for d in first:
        greet(d)

    pg[pl.ds(p_pad - 16, 16), :] = jnp.zeros((16, EMB), jnp.bfloat16)
    local = [
        pltpu.make_async_copy(src, dst, local_sem.at[i])
        for i, (src, dst) in enumerate(
            [
                (labels_hbm, labels),
                (q_hbm, qbuf.at[0, pl.ds(0, q_rows)]),
                (p_hbm.reshape(p_rows, EMB), pg.at[pl.ds(0, p_rows)]),
                (counts_hbm, counts),
                (scale_hbm, scale),
                (bias_hbm, bias),
            ]
        )
    ]
    for d in others:
        greet(d)
    for copy in local:
        copy.start()

    local[0].wait()
    row = lax.broadcasted_iota(jnp.int32, (16, EMB), 0)
    lane = lax.broadcasted_iota(jnp.int32, (16, EMB), 1)
    which = (row & 1) * (EMB // QT) + lane // QT
    label = jnp.zeros((16, EMB), jnp.int32)
    for q in range(q_rows // QT):
        label = jnp.where(which == q, labels[q], label)
    qbuf[0, pl.ds(q_rows, 16), :] = jnp.where(row < 2, label >> 1, label & 1).astype(jnp.float32).astype(jnp.bfloat16)

    local[1].wait()
    pl.semaphore_wait(barrier, len(first) + len(others))

    def q_copy(slot):
        return pltpu.make_async_remote_copy(
            qbuf.at[0], qbuf.at[slot], q_send.at[slot], q_recv.at[slot],
            device_id=(peer(1 << bits[slot - 1]),), device_id_type=MESH,
        )

    for slot in (3, 4, 2, 1):
        q_copy(slot).start()

    def vouch(sem, offsets):
        for d in offsets:
            pl.semaphore_signal(sem, inc=1, device_id=(peer(d),), device_id_type=MESH)

    vouch(column_sem, column)

    group_row = lax.broadcasted_iota(jnp.int32, (q_rows, q_rows), 0) // QT
    group_col = lax.broadcasted_iota(jnp.int32, (q_rows, q_rows), 1) // QT
    ones[...] = jnp.where(group_row == group_col, 1.0, 0.0).astype(jnp.bfloat16)
    sub = lax.broadcasted_iota(jnp.int32, (8, q_rows), 0)
    parity = sub & 1
    for copy in local[2:]:
        copy.wait()
    limit = 2 * jnp.where(parity == 0, counts[0], counts[1]) - sub

    for c in range(CHUNKS):
        pgt[c] = pg[pl.ds(c * chunk, chunk), :].astype(jnp.float32).T.astype(jnp.bfloat16)

    gp_out[...] = jnp.zeros_like(gp_out)

    def all_rows(vec, op):
        vec = op(vec, pltpu.roll(vec, 2, 0))
        return op(vec, pltpu.roll(vec, 4, 0))

    def forward(k):
        q = qbuf[k, pl.ds(0, q_rows), :]
        top = jnp.full((8, q_rows), -jnp.inf, jnp.float32)
        for c in range(CHUNKS):
            x = lax.dot_general(
                pg[pl.ds(c * chunk, chunk), :], q, (((1,), (1,)), ((), ())), preferred_element_type=jnp.float32
            ).reshape(chunk // 8, 8, q_rows)
            if (c + 1) * chunk > 2 * MIN_COUNT:
                start = c * chunk + 8 * lax.broadcasted_iota(jnp.int32, x.shape, 0)
                x = jnp.where(limit[None] > start, x, -jnp.inf)
            xs[k, c] = x
            top = jnp.maximum(top, jnp.max(x, axis=0))
        top = all_rows(top, jnp.maximum)
        tops[k] = top
        total = jnp.zeros((8, q_rows), jnp.float32)
        for c in range(CHUNKS):
            e = jnp.exp2((xs[k, c] - top[None]) * EXP2_SCALE)
            xs[k, c] = e
            total = total + jnp.sum(e, axis=0)
        totals[k] = total

    def scores(blocks):
        parts = []
        total = [all_rows(totals[k], jnp.add) for k in blocks]
        for n, k in enumerate(blocks):
            soft = tops[k] + TAU * jnp.log(total[n])
            hi = soft.astype(jnp.bfloat16).astype(jnp.float32)
            rest = soft - hi
            mid = rest.astype(jnp.bfloat16).astype(jnp.float32)
            parts += [hi, mid, rest - mid]
        if len(parts) % 2:
            parts.append(jnp.zeros_like(parts[0]))
        parts = jnp.concatenate(parts, axis=0).astype(jnp.bfloat16)
        sums = jnp.dot(parts, ones[...], preferred_element_type=jnp.float32).reshape(-1, 8, q_rows)
        loss = jnp.zeros((8, q_rows), jnp.float32)
        for n, k in enumerate(blocks):
            score = sums[3 * n] + sums[3 * n + 1] + sums[3 * n + 2]
            logit = scale[0] * score + bias[0]
            tag = qbuf[k, pl.ds(q_rows, 16), :].astype(jnp.float32)
            block = jnp.concatenate([tag[0:1], tag[1:2]], axis=1)
            page = jnp.concatenate([tag[2:3], tag[3:4]], axis=1)
            positive = (block == me.astype(jnp.float32)) & (page == parity.astype(jnp.float32))
            sign = jnp.where(positive, 1.0, -1.0)
            t = -sign * logit
            decay = jnp.exp(-jnp.abs(t))
            loss = loss + (jnp.maximum(t, 0.0) + jnp.log1p(decay))
            slope = -sign * scale[0] * jnp.where(t >= 0, 1.0, decay) / (1.0 + decay)
            factors[k] = slope / total[n]
        return loss

    def pair(turn, _):
        for k in (2 * turn + 1, 2 * turn + 2):
            pltpu.make_async_copy(qbuf.at[k], qbuf.at[k], q_recv.at[k]).wait()

        @pl.when(turn == 0)
        def _():
            pl.semaphore_wait(column_sem, len(column))
            vouch(core_sem, core)

        forward(2 * turn + 1)
        forward(2 * turn + 2)
        losses[...] += scores((2 * turn + 1, 2 * turn + 2))
        return 0

    forward(0)
    losses[...] = scores((0,))
    lax.fori_loop(0, 2, pair, 0)

    def l_copy(stage, slot):
        return pltpu.make_async_remote_copy(
            lsend.at[stage], lbufs[stage].at[slot], l_send.at[stage], l_recv.at[stage],
            device_id=(peer(groups[stage][slot]),), device_id_type=MESH,
        )

    def l_wait(stage, sem):
        buf = lbufs[stage].at[pl.ds(1, len(groups[stage]) - 1)]
        pltpu.make_async_copy(buf, buf, sem.at[stage]).wait()

    def l_start(stage, v):
        lsend[stage] = v
        lbufs[stage][0] = v
        for slot in order[stage]:
            l_copy(stage, slot).start()

    def tree(v):
        while v.shape[0] > 1:
            half = v.shape[0] // 2
            v = v[:half] + v[half:]
        return v[0]

    loss = jnp.sum(losses[...], axis=0, keepdims=True)
    pl.semaphore_wait(core_sem, len(core))
    l_start(0, loss[:, :EMB] + loss[:, EMB:])

    def backward(step, _):
        k = 4 - step
        q = qbuf[k, pl.ds(0, q_rows), :]
        factor = factors[k]
        grad_q = jnp.zeros((EMB, q_rows), jnp.float32)
        for c in range(CHUNKS):
            coef = (xs[k, c] * factor[None]).reshape(chunk, q_rows).astype(jnp.bfloat16)
            grad_q = grad_q + jnp.dot(pgt[c], coef, preferred_element_type=jnp.float32)
            part = jnp.dot(coef, q, preferred_element_type=jnp.float32)
            here = pl.ds(c * chunk, chunk)

            gp_out[here, :] += part

        @pl.when(k == 0)
        def _():
            gown[...] = grad_q

        @pl.when(k > 0)
        def _():
            gsend[k] = grad_q.astype(jnp.bfloat16)
            target = me
            for slot in range(1, 5):
                target = target + jnp.where(k == slot, flip[bits[slot - 1]], 0)
            pltpu.make_async_remote_copy(
                gsend.at[k], grecv.at[k], g_send.at[k], g_recv.at[k], device_id=(target,), device_id_type=MESH,
            ).start()

        return 0

    lax.fori_loop(0, 5, backward, 0)

    l_wait(0, l_recv)
    l_start(1, tree(l1[...]))
    grad = gown[...]
    for slot in (1, 2, 3, 4):
        pltpu.make_async_copy(grecv.at[slot], grecv.at[slot], g_recv.at[slot]).wait()
        grad = grad + grecv[slot].astype(jnp.float32)
    gq_out[...] = grad.T
    for slot in range(1, 5):
        q_copy(slot).wait_send()
        pltpu.make_async_copy(gsend.at[slot], gsend.at[slot], g_send.at[slot]).wait()
    l_wait(0, l_send)
    l_wait(1, l_recv)
    loss_out[...] = tree(l2[...])
    l_wait(1, l_send)


def finish(loss, gq, gp, loss_out, gq_out, gp_out, total, sem):
    n_page, emb = gp_out.shape[1:]
    flat = gp_out.reshape(gp_out.shape[0] * n_page, emb)
    copies = [
        pltpu.make_async_copy(gp.at[pl.ds(0, flat.shape[0])], flat, sem.at[0]),
        pltpu.make_async_copy(gq, gq_out, sem.at[1]),
        pltpu.make_async_copy(total, loss_out, sem.at[2]),
    ]
    copies[0].start()
    copies[1].start()
    total[0, 0] = jnp.sum(loss[...]) * (1.0 / (4 * QT))
    copies[2].start()
    for copy in copies:
        copy.wait()


def per_device(n_dev, queries, pages, counts, labels, logit_scale, logit_bias):
    n_query, q_tok, emb = queries.shape
    n_page, page_len, _ = pages.shape
    q_rows = n_query * q_tok
    p_rows = n_page * page_len
    p_pad = (p_rows + 16 * CHUNKS - 1) // (16 * CHUNKS) * (16 * CHUNKS)
    sizes = [len(g) for g in loss_groups(n_dev.bit_length() - 1)]
    vmem = pl.BlockSpec(memory_space=pltpu.VMEM)
    hbm = pl.BlockSpec(memory_space=pltpu.HBM)
    bf16, f32 = jnp.bfloat16, jnp.float32
    dma = pltpu.SemaphoreType.DMA
    gp_shape = jax.ShapeDtypeStruct((page_len, n_page, emb), f32)
    gq_shape = jax.ShapeDtypeStruct((q_rows, emb), f32)
    operands = (
        queries.reshape(q_rows, emb),
        jnp.transpose(pages, (1, 0, 2)),
        counts,
        labels,
        logit_scale.reshape(1),
        logit_bias.reshape(1),
    )
    parts = pl.pallas_call(
        lambda *refs: kernel(n_dev, q_rows, p_rows, *refs),
        out_shape=(jax.ShapeDtypeStruct((1, emb), f32), gq_shape, jax.ShapeDtypeStruct((p_pad, emb), f32)),
        in_specs=[hbm] * 6,
        out_specs=(vmem, vmem, vmem),
        scratch_shapes=[
            pltpu.SMEM(counts.shape, jnp.int32),
            pltpu.SMEM(labels.shape, jnp.int32),
            pltpu.SMEM((1,), f32),
            pltpu.SMEM((1,), f32),
            pltpu.VMEM((5, q_rows + 16, emb), bf16),
            pltpu.VMEM((p_pad, emb), bf16),
            pltpu.VMEM((CHUNKS, emb, p_pad // CHUNKS), bf16),
            pltpu.VMEM((5, CHUNKS, p_pad // (8 * CHUNKS), 8, q_rows), f32),
            pltpu.VMEM((5, 8, q_rows), f32),
            pltpu.VMEM((5, 8, q_rows), f32),
            pltpu.VMEM((5, 8, q_rows), f32),
            pltpu.VMEM((8, q_rows), f32),
            pltpu.VMEM((emb, q_rows), f32),
            pltpu.VMEM((5, emb, q_rows), bf16),
            pltpu.VMEM((5, emb, q_rows), bf16),
            pltpu.VMEM((q_rows, q_rows), bf16),
            pltpu.VMEM((2, 1, emb), f32),
            *[pltpu.VMEM((n, 1, emb), f32) for n in sizes],
            dma((6,)),
            dma((5,)),
            dma((5,)),
            dma((5,)),
            dma((5,)),
            dma((2,)),
            dma((2,)),
            pltpu.SemaphoreType.REGULAR,
            pltpu.SemaphoreType.REGULAR,
        ],
        compiler_params=pltpu.CompilerParams(
            collective_id=0, has_side_effects=True, vmem_limit_bytes=40 * 1024 * 1024
        ),
    )(*[pltpu.with_memory_space_constraint(x, pltpu.HBM) for x in operands[:4]], *operands[4:])
    loss, grad_q, grad_p = pl.pallas_call(
        finish,
        out_shape=(jax.ShapeDtypeStruct((1, 1), f32), gq_shape, gp_shape),
        in_specs=[vmem] * 3,
        out_specs=(hbm, hbm, hbm),
        scratch_shapes=[pltpu.SMEM((1, 1), f32), dma((3,))],
        compiler_params=pltpu.CompilerParams(vmem_limit_bytes=16 * 1024 * 1024),
    )(*parts)
    return loss.reshape(()), grad_q.reshape(n_query, q_tok, emb), jnp.transpose(grad_p, (1, 0, 2))


def solution(mesh):
    n_dev = mesh.shape["dp"]
    placed = (P("dp", None, None), P("dp", None, None), P("dp"), P("dp"), P(), P())
    return jax.shard_map(
        lambda *args: per_device(n_dev, *args),
        mesh=mesh,
        in_specs=placed,
        out_specs=(P(), P("dp", None, None), P("dp", None, None)),
        check_vma=False,
    )
```
